256 devices in a mesh: gz: 16 (over z_lo, x, core), gy: 16 (over z_hi, y).
Axes of the slice: x: 4, y: 4, z: 8 (z_hi: 4, z_lo: 2; z = z_hi * 2 + z_lo), core: 2. Of those that a mesh axis runs over, the one named last changes fastest.
Arguments:
- features: bfloat16 [112, 112, 2688], P('gz', 'gy'), may hold values from -6 to 6
- region: int32 [112, 112, 28], P('gz', 'gy'), may hold values from 0 to 3
- labels: int32 [112, 112, 28], P('gz', 'gy'), may hold values from 0 to 13
- attn_gain: float32 [96], replicated, may hold values from 0.25 to 1.75
- qkv_weight: bfloat16 [96, 288], replicated, may hold values from -0.625 to 0.625
- proj_weight: bfloat16 [96, 96], replicated, may hold values from -0.625 to 0.625
- mlp_gain: float32 [96], replicated, may hold values from 0.25 to 1.75
- up_weight: bfloat16 [96, 384], replicated, may hold values from -0.625 to 0.625
- down_weight: bfloat16 [384, 96], replicated, may hold values from -0.3125 to 0.3125
- head_weight: bfloat16 [96, 14], replicated, may hold values from -0.625 to 0.625
Outputs:
- grad_features: bfloat16 [112, 112, 2688], P('gz', 'gy')
The draws below stay inside these ranges and needn't reach their ends.
All inputs are finite; a program needn't handle non-finite values.
Results may differ from the reference program's by a relative error of at most 0.022.
Values may be sent and summed in bfloat16 or wider, within the bound.
No kernel may reach another device: no remote copies, remote signals or barrier semaphores. Data moves between devices by JAX's collectives and lax.ppermute only.
A program may use at most 128 MiB of HBM per device.

```python
import jax
import jax.numpy as jnp
from jax import lax

C = 96
HEADS = 6
HID = 384
CLASSES = 14
WIN = 7
SHIFT = 3
NX = 28
NZ = 112
NY = 112
N_GZ = 16
N_GY = 16


def with_ends(result, rng, least, high):
    index_at = [jax.random.randint(jax.random.fold_in(rng, axis), (), 0, length) for axis, length in enumerate(result.shape)]
    widest = result.shape.index(max(result.shape))
    next_to = index_at[:widest] + [(index_at[widest] + 1) % result.shape[widest]] + index_at[widest + 1:]
    return result.at[tuple(index_at)].set(least).at[tuple(next_to)].set(high)


def level_of(key, shape, pieces, least, largest):
    def one(dim, blocks):
        draws = jax.random.uniform(jax.random.fold_in(jax.random.fold_in(key, 6), dim), (blocks,), jnp.float32, least / len(pieces), largest / len(pieces))
        return jnp.repeat(jnp.exp(draws), shape[dim] // blocks).reshape((-1,) + (1,) * (len(shape) - dim - 1))

    loudness = one(*pieces[0])
    for cut in pieces[1:]:
        loudness = loudness * one(*cut)
    return loudness


def centred(own_key, extent, width, most, split=(), kind=jnp.bfloat16):
    values = width * jax.random.normal(own_key, extent, jnp.float32)
    if split:
        values = values * level_of(own_key, extent, split, -0.22, 0.18)
    return jnp.clip(values, -most, most).astype(kind)


def setup_inputs(seed: int = 0) -> dict:
    arg_keys = jax.random.split(jax.random.key(seed), 11)
    return {
        "features": centred(arg_keys[0], (NZ, NY, NX * C), 1.0, 6.0, ((0, 16), (1, 16))),
        "region": with_ends(jax.random.randint(arg_keys[1], (NZ, NY, NX), 0, 4), jax.random.fold_in(arg_keys[1], 1), 0, 3).astype(jnp.int32),
        "labels": with_ends(jax.random.randint(arg_keys[2], (NZ, NY, NX), 0, CLASSES), jax.random.fold_in(arg_keys[2], 1), 0, CLASSES - 1).astype(jnp.int32),
        "attn_gain": jnp.clip(1.0 + 0.15 * jax.random.normal(arg_keys[3], (C,), jnp.float32), 0.25, 1.75),
        "qkv_weight": centred(arg_keys[4], (C, 3 * C), C ** -0.5, 0.625),
        "proj_weight": centred(arg_keys[5], (C, C), C ** -0.5, 0.625),
        "mlp_gain": jnp.clip(1.0 + 0.15 * jax.random.normal(arg_keys[6], (C,), jnp.float32), 0.25, 1.75),
        "up_weight": centred(arg_keys[7], (C, HID), C ** -0.5, 0.625),
        "down_weight": centred(arg_keys[8], (HID, C), HID ** -0.5, 0.3125),
        "head_weight": centred(arg_keys[9], (C, CLASSES), C ** -0.5, 0.625),
    }


def product(form, left, right):
    return jnp.einsum(form, left.astype(jnp.float32), right.astype(jnp.float32))

def norm_rows(values, gain):
    center = values - lax.optimization_barrier(jnp.mean(values, axis=1, keepdims=True))
    spread = lax.optimization_barrier(jnp.mean(center * center, axis=1, keepdims=True))
    return (center * lax.rsqrt(spread + 1e-05) * gain[None, :, None]).astype(jnp.bfloat16)

def attend(queries, key_part, value_part, region_ids):
    channels, token_count = queries.shape
    head_dim = channels // HEADS
    query_heads = queries.reshape(HEADS, head_dim, token_count)
    key_heads = key_part.reshape(HEADS, head_dim, token_count)
    value_heads = value_part.reshape(HEADS, head_dim, token_count)
    scores = product('hdq,hdk->hqk', query_heads, key_heads) * head_dim ** (-0.5)
    allowed = region_ids[:, None] == region_ids[None, :]
    scores = jnp.where(allowed[None], scores, -1000000000.0)
    row_max = lax.stop_gradient(lax.optimization_barrier(jnp.max(scores, axis=2, keepdims=True)))
    raised = jnp.exp(scores - row_max)
    weights_soft = (raised / lax.optimization_barrier(jnp.sum(raised, axis=2, keepdims=True))).astype(jnp.bfloat16)
    mixed_out = product('hqk,hdk->hdq', weights_soft, value_heads)
    return mixed_out.reshape(channels, token_count).astype(jnp.bfloat16)

def block_loss(field_in, region, labels, attn_gain, qkv_weight, proj_weight, mlp_gain, up_weight, down_weight, head_weight):
    depth_count, row_count, merged = field_in.shape
    columns = region.shape[2]
    channels = merged // columns
    windows = columns // WIN
    volume = jnp.roll(field_in.reshape(depth_count, row_count, columns, channels), -SHIFT, axis=2)
    tokens = volume.reshape(depth_count, row_count, windows, WIN, channels).transpose(2, 4, 0, 1, 3)
    tokens = tokens.reshape(windows, channels, depth_count * row_count * WIN)
    region_w = region.reshape(depth_count, row_count, windows, WIN).transpose(2, 0, 1, 3).reshape(windows, -1)
    labels_w = labels.reshape(depth_count, row_count, windows, WIN).transpose(2, 0, 1, 3).reshape(windows, -1)
    normed = norm_rows(tokens.astype(jnp.float32), attn_gain)
    mixed_qkv = product('nct,cf->nft', normed, qkv_weight).astype(jnp.bfloat16)
    queries = mixed_qkv[:, :channels]
    key_part = mixed_qkv[:, channels:2 * channels]
    value_part = mixed_qkv[:, 2 * channels:]
    attended = lax.map(lambda window_parts: attend(*window_parts), (queries, key_part, value_part, region_w))
    projected = product('nct,cf->nft', attended, proj_weight)
    hidden = tokens.astype(jnp.float32) + projected
    normed_two = norm_rows(hidden, mlp_gain)
    raised = product('nct,cf->nft', normed_two, up_weight)
    expanded = jax.nn.gelu(raised, approximate=False).astype(jnp.bfloat16)
    output = hidden + product('nft,fc->nct', expanded, down_weight)
    logits = product('nct,ck->nkt', output.astype(jnp.bfloat16), head_weight)
    log_total = jax.nn.logsumexp(logits, axis=1)
    classes = jnp.arange(logits.shape[1], dtype=jnp.int32)
    picked = lax.optimization_barrier(jnp.sum(jnp.where(labels_w[:, None, :] == classes[None, :, None], logits, 0.0), axis=1))
    return jnp.sum(log_total - picked)

def split_blocks(array):
    trailing = array.shape[2]
    return array.reshape(N_GZ, WIN, N_GY, WIN, trailing).transpose(0, 2, 1, 3, 4).reshape(N_GZ * N_GY, WIN, WIN, trailing)

def reference(features, region, labels, attn_gain, qkv_weight, proj_weight, mlp_gain, up_weight, down_weight, head_weight):
    merged = features.shape[2]
    rolled = jnp.roll(features, (-SHIFT, -SHIFT), axis=(0, 1))
    loss_scale = 1.0 / (NZ * NY * NX)
    weights = (attn_gain, qkv_weight, proj_weight, mlp_gain, up_weight, down_weight, head_weight)

    def visit(piece_set):
        field_in, region_part, label_part = piece_set

        def local_loss(field_value):
            return block_loss(field_value, region_part, label_part, *weights)
        part_loss, pullback = jax.vjp(local_loss, field_in)
        cotangents = pullback(jnp.asarray(loss_scale, part_loss.dtype))
        return cotangents[0]
    grad_blocks = lax.map(visit, (split_blocks(rolled), split_blocks(region), split_blocks(labels)))
    grad_field = grad_blocks.reshape(N_GZ, N_GY, WIN, WIN, merged).transpose(0, 2, 1, 3, 4).reshape(NZ, NY, merged)
    grad_field = jnp.roll(grad_field, (SHIFT, SHIFT), axis=(0, 1))
    return grad_field
```

```python
import functools

import jax
import jax.numpy as jnp
from jax import lax
from jax.experimental import pallas as pl
from jax.experimental.pallas import tpu as pltpu
from jax.sharding import PartitionSpec as P

C = 96
HEADS = 6
HEAD = 16
HID = 384
CLASSES = 14
WIN = 7
SHIFT = 3
KEEP = WIN - SHIFT
NX = 28
WINDOWS = 4
TOKENS = 343
LANES = 384
SLOTS = 64
WIDE = NX * C
FAR = -(2.0**30)
LOG2E = 1.4426950408889634
LN2 = 0.6931471805599453
BF = jnp.bfloat16
F32 = jnp.float32


def nn(a, b):
    return lax.dot_general(a, b, (((1,), (0,)), ((), ())), preferred_element_type=F32)


def nt(a, b):
    return lax.dot_general(a, b, (((1,), (1,)), ((), ())), preferred_element_type=F32)


def piece_rows(cells, depths, rows):
    parts = [cells[d][rows[0] : rows[1]] for d in depths]
    used = len(depths) * (rows[1] - rows[0])
    if used < 16:
        parts.append(jnp.zeros((16 - used, parts[0].shape[1]), parts[0].dtype))
    return jnp.concatenate(parts, axis=0)


def cut_kernel(f_ref, a_ref, b_ref, c_ref, d_ref):
    cells = [f_ref[d].astype(F32) for d in range(WIN)]
    low, high = range(SHIFT), range(SHIFT, WIN)
    a_ref[...] = piece_rows(cells, high, (SHIFT, WIN)).astype(BF)
    b_ref[...] = piece_rows(cells, low, (SHIFT, WIN)).astype(BF)
    c_ref[...] = piece_rows(cells, high, (0, SHIFT)).astype(BF)
    d_ref[...] = piece_rows(cells, low, (0, SHIFT)).astype(BF)


def join_kernel(a_ref, b_ref, c_ref, d_ref, out_ref):
    a = a_ref[...].astype(F32)
    b = b_ref[...].astype(F32)
    c = c_ref[...].astype(F32)
    d = d_ref[...].astype(F32)
    for i in range(WIN):
        if i < SHIFT:
            left, right, k = d, b, i
        else:
            left, right, k = c, a, i - SHIFT
        rows = [left[SHIFT * k : SHIFT * k + SHIFT], right[KEEP * k : KEEP * k + KEEP]]
        out_ref[i] = jnp.concatenate(rows, axis=0).astype(BF)


def selector():
    token = lax.broadcasted_iota(jnp.int32, (1, LANES), 1)
    column = (token * 1338) >> 16
    cell = token - 49 * column
    slot = 64 * column + cell + 4 * (cell >= 28).astype(jnp.int32) + 4 * (cell >= 40).astype(jnp.int32)
    slot = jnp.where(token < TOKENS, slot, -1)
    place = lax.broadcasted_iota(jnp.int32, (WIN * SLOTS, LANES), 0)
    return (place == slot).astype(F32).astype(BF)


def by_slots(values):
    cells = [values[d] for d in range(WIN)]
    low, high = range(KEEP), range(KEEP, WIN)
    return jnp.concatenate(
        [
            piece_rows(cells, low, (0, KEEP)),
            piece_rows(cells, high, (0, KEEP)),
            piece_rows(cells, low, (KEEP, WIN)),
            piece_rows(cells, high, (KEEP, WIN)),
        ],
        axis=0,
    )


def turned(values):
    return values.astype(F32).T.astype(BF)


def ready_kernel(
    region_ref, labels_ref, g1_ref, g2_ref, qkv_ref, proj_ref, up_ref, down_ref, head_ref,
    ids_ref, sel_ref, gain1_ref, gain2_ref, qkvt_ref, projt_ref, upt_ref, downt_ref, headt_ref, heads_ref,
):
    sel = selector()
    sel_ref[...] = sel
    rows = []
    for ref in (region_ref, labels_ref):
        flat = by_slots(ref[...].astype(F32)).T
        for w in range(WINDOWS):
            rows.append(jnp.concatenate([flat[WIN * w + c : WIN * w + c + 1] for c in range(WIN)], axis=1))
    ids = nn(jnp.concatenate(rows, axis=0).astype(BF), sel)
    token = lax.broadcasted_iota(jnp.int32, ids.shape, 1)
    row = lax.broadcasted_iota(jnp.int32, ids.shape, 0)
    ids_ref[...] = jnp.where(token < TOKENS, ids, jnp.where(row < WINDOWS, 4.0, -1.0))
    for ref, out in ((g1_ref, gain1_ref), (g2_ref, gain2_ref)):
        out[...] = jnp.broadcast_to(ref[...], (128, C)).T
    qkvt_ref[...] = turned(qkv_ref[...])
    projt_ref[...] = turned(proj_ref[...])
    upt_ref[...] = turned(up_ref[...])
    downt_ref[...] = turned(down_ref[...])
    head = head_ref[...].astype(F32)
    head = jnp.concatenate([head, jnp.zeros((C, 2), F32)], axis=1)
    headt_ref[...] = head.T.astype(BF)
    heads_ref[...] = head.astype(BF)


def norm(values, gain):
    center = values - jnp.mean(values, axis=0, keepdims=True)
    inverse = lax.rsqrt(jnp.mean(center * center, axis=0, keepdims=True) + 1e-5)
    unit = center * inverse
    return unit, inverse, (unit * gain).astype(BF)


def norm_back(cotangent, unit, inverse, gain):
    scaled = cotangent * gain
    middle = jnp.mean(scaled, axis=0, keepdims=True)
    along = jnp.mean(scaled * unit, axis=0, keepdims=True)
    return inverse * (scaled - middle - unit * along)


def headed(head, rows, extra):
    parts = []
    if head:
        parts.append(jnp.zeros((HEAD * head, LANES), BF))
    parts.append(rows)
    if head < HEADS - 1:
        parts.append(jnp.zeros((C - HEAD * head - HEAD, LANES), BF))
    return jnp.concatenate(parts + [extra, jnp.zeros((16, LANES), BF)], axis=0)


def main_kernel(
    scale,
    a_ref, b_ref, c_ref, d_ref, ids_ref, sel_ref, gain1_ref, gain2_ref,
    qkv_ref, qkvt_ref, proj_ref, projt_ref, up_ref, upt_ref, down_ref, downt_ref, head_ref, headt_ref,
    oa_ref, ob_ref, oc_ref, od_ref,
    x_ref, grad_ref, e_ref, slope_ref, sides_ref,
):
    sel = sel_ref[...]
    rows = jnp.concatenate([r[...].astype(F32) for r in (a_ref, b_ref, c_ref, d_ref)], axis=0)
    tall = rows.T
    for w in range(WINDOWS):
        cols = [(WIN * w + SHIFT + c) % NX for c in range(WIN)]
        wide = jnp.concatenate([tall[C * c : C * c + C] for c in cols], axis=1).astype(BF)
        x_ref[w] = nn(wide, sel).astype(F32)

    def window(w, carry):
        gain1 = jnp.concatenate([gain1_ref[...]] * 3, axis=1)
        gain2 = jnp.concatenate([gain2_ref[...]] * 3, axis=1)
        x = x_ref[w]
        unit1, inverse1, normed1 = norm(x, gain1)
        region = ids_ref[pl.ds(w, 1), :]
        labels = ids_ref[pl.ds(w + WINDOWS, 1), :]
        qkv = nn(qkvt_ref[...], normed1)
        queries = (qkv[:C] * (0.25 * LOG2E)).astype(BF)
        keys = qkv[C : 2 * C].astype(BF)
        values = qkv[2 * C :].astype(BF)
        index = lax.broadcasted_iota(jnp.int32, (16, LANES), 0)
        same = index.astype(F32) == region
        key_side = same.astype(F32).astype(BF)
        query_side = jnp.where(same | (index > 4), 0.0, FAR).astype(BF)
        ones = jnp.where(index < 2, 1.0, 0.0).astype(BF)
        blank = jnp.zeros((16, LANES), BF)
        keys_t = turned(jnp.concatenate([keys, key_side, blank], axis=0))
        values_t = turned(jnp.concatenate([values, ones, blank], axis=0))
        attended = []
        inverse_sums = []
        for h in range(HEADS):
            own = slice(HEAD * h, HEAD * h + HEAD)
            scores = nn(keys_t, headed(h, queries[own], query_side))
            top = jnp.max(scores, axis=0, keepdims=True)
            raised = jnp.exp2(scores - top).astype(BF)
            e_ref[h] = raised
            mixed = nn(jnp.concatenate([values[own], ones], axis=0), raised)
            inverse_sum = 1.0 / mixed[HEAD : HEAD + 1]
            inverse_sums.append(inverse_sum)
            attended.append((mixed[:HEAD] * inverse_sum).astype(BF))
        hidden = x + nn(projt_ref[...], jnp.concatenate(attended, axis=0))
        unit2, inverse2, normed2 = norm(hidden, gain2)
        output = hidden
        for j in range(3):
            part = slice(128 * j, 128 * j + 128)
            raised = nn(upt_ref[part, :], normed2)
            below = 0.5 + 0.5 * lax.erf(raised * (0.5**0.5))
            bell = jnp.exp(-0.5 * raised * raised) * 0.3989422804014327
            slope_ref[part, :] = below + raised * bell
            output = output + nn(downt_ref[:, part], (raised * below).astype(BF))
        logits = nn(headt_ref[...], output.astype(BF))
        kind = lax.broadcasted_iota(jnp.int32, (16, LANES), 0)
        logits = jnp.where(kind < CLASSES, logits, -1e30)
        powers = jnp.exp(logits - jnp.max(logits, axis=0, keepdims=True))
        soft = powers / jnp.sum(powers, axis=0, keepdims=True)
        at_label = (kind.astype(F32) == labels).astype(F32)
        d_logits = jnp.where(labels >= 0.0, (soft - at_label) * scale, 0.0)
        d_output = nn(head_ref[...], d_logits.astype(BF)).astype(BF)
        d_normed2 = jnp.zeros((C, LANES), F32)
        for j in range(3):
            part = slice(128 * j, 128 * j + 128)
            d_expanded = nn(down_ref[part, :], d_output)
            d_raised = (d_expanded * slope_ref[part, :]).astype(BF)
            d_normed2 = d_normed2 + nn(up_ref[:, part], d_raised)
        d_hidden = d_output.astype(F32) + norm_back(d_normed2, unit2, inverse2, gain2)
        d_attended = nn(proj_ref[...], d_hidden.astype(BF))
        d_queries = []
        d_keys = []
        d_values = []
        for h in range(HEADS):
            own = slice(HEAD * h, HEAD * h + HEAD)
            d_mixed = (d_attended[own] * inverse_sums[h]).astype(BF)
            along = -jnp.sum(d_mixed.astype(F32) * attended[h].astype(F32), axis=0, keepdims=True)
            coarse = along.astype(BF).astype(F32)
            extra = jnp.where(index == 0, coarse, jnp.where(index == 1, along - coarse, 0.0)).astype(BF)
            raised = e_ref[h]
            d_scores = (raised.astype(F32) * nn(values_t, headed(h, d_mixed, extra))).astype(BF)
            d_values.append(nt(d_mixed, raised))
            d_queries.append(nn(keys[own], d_scores) * 0.25)
            d_keys.append(nt(queries[own], d_scores) * LN2)
        d_qkv = jnp.concatenate(d_queries + d_keys + d_values, axis=0).astype(BF)
        d_normed1 = nn(qkv_ref[...], d_qkv)
        grad_ref[w] = (d_hidden + norm_back(d_normed1, unit1, inverse1, gain1)).astype(BF)
        return carry

    lax.fori_loop(0, WINDOWS, window, 0)
    blocks = [None] * NX
    for w in range(WINDOWS):
        wide = nt(grad_ref[w], sel)
        for c in range(WIN):
            blocks[(WIN * w + SHIFT + c) % NX] = wide[:, SLOTS * c : SLOTS * c + SLOTS]
    rows = jnp.concatenate(blocks, axis=0).T
    for k, ref in enumerate((oa_ref, ob_ref, oc_ref, od_ref)):
        ref[...] = rows[16 * k : 16 * k + 16].astype(BF)


VMEM = pl.BlockSpec(memory_space=pltpu.VMEM)
PIECE = jax.ShapeDtypeStruct((16, WIDE), BF)


def cut(features):
    return pl.pallas_call(cut_kernel, out_shape=[PIECE] * 4, in_specs=[VMEM], out_specs=[VMEM] * 4)(features)


def join(*pieces):
    out = jax.ShapeDtypeStruct((WIN, WIN, WIDE), BF)
    return pl.pallas_call(join_kernel, out_shape=out, in_specs=[VMEM] * 4, out_specs=VMEM)(*pieces)


def ready(region, labels, attn_gain, mlp_gain, qkv_weight, proj_weight, up_weight, down_weight, head_weight):
    S = jax.ShapeDtypeStruct
    out = [
        S((8, LANES), F32), S((WIN * SLOTS, LANES), BF), S((C, 128), F32), S((C, 128), F32),
        S((3 * C, C), BF), S((C, C), BF), S((HID, C), BF), S((C, HID), BF), S((16, C), BF), S((C, 16), BF),
    ]
    return pl.pallas_call(ready_kernel, out_shape=out, in_specs=[VMEM] * 9, out_specs=[VMEM] * 10)(
        region, labels, attn_gain.reshape(1, C), mlp_gain.reshape(1, C),
        qkv_weight, proj_weight, up_weight, down_weight, head_weight,
    )


def gradient(pieces, prepared, weights, scale):
    ids, sel, gain1, gain2, qkv_t, proj_t, up_t, down_t, head_t, head = prepared
    qkv_weight, proj_weight, up_weight, down_weight = weights
    return pl.pallas_call(
        functools.partial(main_kernel, scale),
        out_shape=[PIECE] * 4,
        in_specs=[VMEM] * 18,
        out_specs=[VMEM] * 4,
        scratch_shapes=[
            pltpu.VMEM((WINDOWS, C, LANES), F32),
            pltpu.VMEM((WINDOWS, C, LANES), BF),
            pltpu.VMEM((HEADS, LANES, LANES), BF),
            pltpu.VMEM((HID, LANES), F32),
            pltpu.VMEM((16, LANES), F32),
        ],
        compiler_params=pltpu.CompilerParams(vmem_limit_bytes=48 * 2**20),
    )(
        *pieces, ids, sel, gain1, gain2, qkv_weight, qkv_t, proj_weight, proj_t,
        up_weight, up_t, down_weight, down_t, head, head_t,
    )


def moved(piece, axes, steps):
    sizes = [lax.axis_size(a) for a in axes]
    route = []
    if len(axes) == 1:
        (n,) = sizes
        route = [((i - steps) % n, i) for i in range(n)]
    else:
        n, m = sizes
        for i in range(n):
            for j in range(m):
                route.append((((i - steps) % n) * m + (j - steps) % m, i * m + j))
    return lax.ppermute(piece, axes if len(axes) > 1 else axes[0], route)


ROADS = (("gz",), ("gy",), ("gz", "gy"))


def body(
    features, region, labels, attn_gain, qkv_weight, proj_weight, mlp_gain, up_weight, down_weight, head_weight,
):
    own, *away = cut(features)
    arrived = [moved(piece, road, -1) for piece, road in zip(away, ROADS)]
    prepared = ready(
        region, labels, attn_gain, mlp_gain, qkv_weight, proj_weight, up_weight, down_weight, head_weight
    )
    scale = 1.0 / (WIN * WIN * NX * lax.axis_size("gz") * lax.axis_size("gy"))
    own, *away = gradient((own, *arrived), prepared, (qkv_weight, proj_weight, up_weight, down_weight), scale)
    arrived = [moved(piece, road, 1) for piece, road in zip(away, ROADS)]
    return join(own, *arrived)


def solution(mesh):
    cells = P("gz", "gy", None)
    in_specs = (cells, cells, cells) + (P(),) * 7
    return jax.shard_map(body, mesh=mesh, in_specs=in_specs, out_specs=cells, check_vma=False)
```

```python
import functools

import jax
import jax.numpy as jnp
from jax import lax
from jax.experimental import pallas as pl
from jax.experimental.pallas import tpu as pltpu
from jax.sharding import PartitionSpec as P

C = 96
HEADS = 6
HEAD = 16
HID = 384
CLASSES = 14
WIN = 7
SHIFT = 3
KEEP = WIN - SHIFT
NX = 28
WINDOWS = 4
TOKENS = 343
LANES = 384
SLOTS = 64
WIDE = NX * C
FAR = -(2.0**30)
LOG2E = 1.4426950408889634
LN2 = 0.6931471805599453
BF = jnp.bfloat16
F32 = jnp.float32


def nn(a, b):
    return lax.dot_general(a, b, (((1,), (0,)), ((), ())), preferred_element_type=F32)


def nt(a, b):
    return lax.dot_general(a, b, (((1,), (1,)), ((), ())), preferred_element_type=F32)


def piece_rows(cells, depths, rows):
    parts = [cells[d][rows[0] : rows[1]] for d in depths]
    used = len(depths) * (rows[1] - rows[0])
    if used < 16:
        parts.append(jnp.zeros((16 - used, parts[0].shape[1]), parts[0].dtype))
    return jnp.concatenate(parts, axis=0)


def cut_kernel(f_ref, a_ref, b_ref, c_ref, d_ref):
    cells = [f_ref[d].astype(F32) for d in range(WIN)]
    low, high = range(SHIFT), range(SHIFT, WIN)
    a_ref[...] = piece_rows(cells, high, (SHIFT, WIN)).astype(BF)
    b_ref[...] = piece_rows(cells, low, (SHIFT, WIN)).astype(BF)
    c_ref[...] = piece_rows(cells, high, (0, SHIFT)).astype(BF)
    d_ref[...] = piece_rows(cells, low, (0, SHIFT)).astype(BF)


def join_kernel(a_ref, b_ref, c_ref, d_ref, out_ref):
    a = a_ref[...].astype(F32)
    b = b_ref[...].astype(F32)
    c = c_ref[...].astype(F32)
    d = d_ref[...].astype(F32)
    for i in range(WIN):
        if i < SHIFT:
            left, right, k = d, b, i
        else:
            left, right, k = c, a, i - SHIFT
        rows = [left[SHIFT * k : SHIFT * k + SHIFT], right[KEEP * k : KEEP * k + KEEP]]
        out_ref[i] = jnp.concatenate(rows, axis=0).astype(BF)


def selector():
    token = lax.broadcasted_iota(jnp.int32, (1, LANES), 1)
    column = (token * 1338) >> 16
    cell = token - 49 * column
    slot = 64 * column + cell + 4 * (cell >= 28).astype(jnp.int32) + 4 * (cell >= 40).astype(jnp.int32)
    slot = jnp.where(token < TOKENS, slot, -1)
    place = lax.broadcasted_iota(jnp.int32, (WIN * SLOTS, LANES), 0)
    return (place == slot).astype(F32).astype(BF)


def by_slots(values):
    cells = [values[d] for d in range(WIN)]
    low, high = range(KEEP), range(KEEP, WIN)
    return jnp.concatenate(
        [
            piece_rows(cells, low, (0, KEEP)),
            piece_rows(cells, high, (0, KEEP)),
            piece_rows(cells, low, (KEEP, WIN)),
            piece_rows(cells, high, (KEEP, WIN)),
        ],
        axis=0,
    )


def turned(values):
    return values.astype(F32).T.astype(BF)


def ready_kernel(
    region_ref, labels_ref, g1_ref, g2_ref, qkv_ref, proj_ref, up_ref, downt_ref, head_ref,
    ids_ref, sel_ref, gain1_ref, gain2_ref, qkvt_ref, projt_ref, upt_ref, down_ref, headt_ref, heads_ref,
):
    sel = selector()
    sel_ref[...] = sel
    rows = []
    for ref in (region_ref, labels_ref):
        flat = by_slots(ref[...].astype(F32)).T
        for w in range(WINDOWS):
            rows.append(jnp.concatenate([flat[WIN * w + c : WIN * w + c + 1] for c in range(WIN)], axis=1))
    ids = nn(jnp.concatenate(rows, axis=0).astype(BF), sel)
    token = lax.broadcasted_iota(jnp.int32, ids.shape, 1)
    row = lax.broadcasted_iota(jnp.int32, ids.shape, 0)
    ids_ref[...] = jnp.where(token < TOKENS, ids, jnp.where(row < WINDOWS, 4.0, -1.0))
    for ref, out in ((g1_ref, gain1_ref), (g2_ref, gain2_ref)):
        out[...] = jnp.broadcast_to(ref[...], (128, C)).T
    qkvt_ref[...] = turned(qkv_ref[...])
    projt_ref[...] = turned(proj_ref[...])
    upt_ref[...] = turned(up_ref[...])
    down_ref[...] = turned(downt_ref[...])
    head = jnp.concatenate([head_ref[...].astype(F32), jnp.zeros((2, C), F32)], axis=0)
    headt_ref[...] = head.astype(BF)
    heads_ref[...] = head.T.astype(BF)


def norm(values, gain):
    center = values - jnp.mean(values, axis=0, keepdims=True)
    inverse = lax.rsqrt(jnp.mean(center * center, axis=0, keepdims=True) + 1e-5)
    unit = center * inverse
    return unit, inverse, (unit * gain).astype(BF)


def norm_back(cotangent, unit, inverse, gain):
    scaled = cotangent * gain
    middle = jnp.mean(scaled, axis=0, keepdims=True)
    along = jnp.mean(scaled * unit, axis=0, keepdims=True)
    return inverse * (scaled - middle - unit * along)


def headed(head, rows, extra):
    parts = []
    if head:
        parts.append(jnp.zeros((HEAD * head, LANES), BF))
    parts.append(rows)
    if head < HEADS - 1:
        parts.append(jnp.zeros((C - HEAD * head - HEAD, LANES), BF))
    return jnp.concatenate(parts + [extra, jnp.zeros((16, LANES), BF)], axis=0)


def main_kernel(
    scale,
    a_ref, b_ref, c_ref, d_ref, ids_ref, sel_ref, gain1_ref, gain2_ref,
    qkv_ref, qkvt_ref, proj_ref, projt_ref, up_ref, upt_ref, down_ref, downt_ref, head_ref, headt_ref,
    oa_ref, ob_ref, oc_ref, od_ref,
    x_ref, grad_ref, e_ref, slope_ref, sides_ref,
):
    sel = sel_ref[...]
    rows = jnp.concatenate([r[...].astype(F32) for r in (a_ref, b_ref, c_ref, d_ref)], axis=0)
    tall = rows.T
    for w in range(WINDOWS):
        cols = [(WIN * w + SHIFT + c) % NX for c in range(WIN)]
        wide = jnp.concatenate([tall[C * c : C * c + C] for c in cols], axis=1).astype(BF)
        x_ref[w] = nn(wide, sel).astype(F32)

    def window(w, carry):
        gain1 = jnp.concatenate([gain1_ref[...]] * 3, axis=1)
        gain2 = jnp.concatenate([gain2_ref[...]] * 3, axis=1)
        x = x_ref[w]
        unit1, inverse1, normed1 = norm(x, gain1)
        region = ids_ref[pl.ds(w, 1), :]
        labels = ids_ref[pl.ds(w + WINDOWS, 1), :]
        qkv = nn(qkvt_ref[...], normed1)
        queries = (qkv[:C] * (0.25 * LOG2E)).astype(BF)
        keys = qkv[C : 2 * C].astype(BF)
        values = qkv[2 * C :].astype(BF)
        index = lax.broadcasted_iota(jnp.int32, (16, LANES), 0)
        same = index.astype(F32) == region
        key_side = same.astype(F32).astype(BF)
        query_side = jnp.where(same | (index > 4), 0.0, FAR).astype(BF)
        ones = jnp.where(index < 2, 1.0, 0.0).astype(BF)
        blank = jnp.zeros((16, LANES), BF)
        keys_t = turned(jnp.concatenate([keys, key_side, blank], axis=0))
        values_t = turned(jnp.concatenate([values, ones, blank], axis=0))
        attended = []
        inverse_sums = []
        for h in range(HEADS):
            own = slice(HEAD * h, HEAD * h + HEAD)
            scores = nn(keys_t, headed(h, queries[own], query_side))
            top = jnp.max(scores, axis=0, keepdims=True)
            raised = jnp.exp2(scores - top).astype(BF)
            e_ref[h] = raised
            mixed = nn(jnp.concatenate([values[own], ones], axis=0), raised)
            inverse_sum = 1.0 / mixed[HEAD : HEAD + 1]
            inverse_sums.append(inverse_sum)
            attended.append((mixed[:HEAD] * inverse_sum).astype(BF))
        hidden = x + nn(projt_ref[...], jnp.concatenate(attended, axis=0))
        unit2, inverse2, normed2 = norm(hidden, gain2)
        output = hidden
        for j in range(3):
            part = slice(128 * j, 128 * j + 128)
            raised = nn(upt_ref[part, :], normed2)
            below = 0.5 + 0.5 * lax.erf(raised * (0.5**0.5))
            bell = jnp.exp(-0.5 * raised * raised) * 0.3989422804014327
            slope_ref[part, :] = below + raised * bell
            output = output + nn(downt_ref[:, part], (raised * below).astype(BF))
        logits = nn(headt_ref[...], output.astype(BF))
        kind = lax.broadcasted_iota(jnp.int32, (16, LANES), 0)
        logits = jnp.where(kind < CLASSES, logits, -1e30)
        powers = jnp.exp(logits - jnp.max(logits, axis=0, keepdims=True))
        soft = powers / jnp.sum(powers, axis=0, keepdims=True)
        at_label = (kind.astype(F32) == labels).astype(F32)
        d_logits = jnp.where(labels >= 0.0, (soft - at_label) * scale, 0.0)
        d_output = nn(head_ref[...], d_logits.astype(BF)).astype(BF)
        d_normed2 = jnp.zeros((C, LANES), F32)
        for j in range(3):
            part = slice(128 * j, 128 * j + 128)
            d_expanded = nn(down_ref[part, :], d_output)
            d_raised = (d_expanded * slope_ref[part, :]).astype(BF)
            d_normed2 = d_normed2 + nn(up_ref[:, part], d_raised)
        d_hidden = d_output.astype(F32) + norm_back(d_normed2, unit2, inverse2, gain2)
        d_attended = nn(proj_ref[...], d_hidden.astype(BF))
        d_queries = []
        d_keys = []
        d_values = []
        for h in range(HEADS):
            own = slice(HEAD * h, HEAD * h + HEAD)
            d_mixed = (d_attended[own] * inverse_sums[h]).astype(BF)
            along = -jnp.sum(d_mixed.astype(F32) * attended[h].astype(F32), axis=0, keepdims=True)
            coarse = along.astype(BF).astype(F32)
            extra = jnp.where(index == 0, coarse, jnp.where(index == 1, along - coarse, 0.0)).astype(BF)
            raised = e_ref[h]
            d_scores = (raised.astype(F32) * nn(values_t, headed(h, d_mixed, extra))).astype(BF)
            d_values.append(nt(d_mixed, raised))
            d_queries.append(nn(keys[own], d_scores) * 0.25)
            d_keys.append(nt(queries[own], d_scores) * LN2)
        d_qkv = jnp.concatenate(d_queries + d_keys + d_values, axis=0).astype(BF)
        d_normed1 = nn(qkv_ref[...], d_qkv)
        grad_ref[w] = (d_hidden + norm_back(d_normed1, unit1, inverse1, gain1)).astype(BF)
        return carry

    lax.fori_loop(0, WINDOWS, window, 0)
    blocks = [None] * NX
    for w in range(WINDOWS):
        wide = nt(grad_ref[w], sel)
        for c in range(WIN):
            blocks[(WIN * w + SHIFT + c) % NX] = wide[:, SLOTS * c : SLOTS * c + SLOTS]
    rows = jnp.concatenate(blocks, axis=0).T
    for k, ref in enumerate((oa_ref, ob_ref, oc_ref, od_ref)):
        ref[...] = rows[16 * k : 16 * k + 16].astype(BF)


VMEM = pl.BlockSpec(memory_space=pltpu.VMEM)
SMALL = pltpu.CompilerParams(vmem_limit_bytes=8 * 2**20)
PIECE = jax.ShapeDtypeStruct((16, WIDE), BF)


def cut(features):
    return pl.pallas_call(cut_kernel, out_shape=[PIECE] * 4, in_specs=[VMEM], out_specs=[VMEM] * 4, compiler_params=SMALL)(features)


def join(*pieces):
    out = jax.ShapeDtypeStruct((WIN, WIN, WIDE), BF)
    return pl.pallas_call(join_kernel, out_shape=out, in_specs=[VMEM] * 4, out_specs=VMEM, compiler_params=SMALL)(*pieces)


def ready(region, labels, attn_gain, mlp_gain, qkv_weight, proj_weight, up_weight, down_weight, head_weight):
    S = jax.ShapeDtypeStruct
    out = [
        S((8, LANES), F32), S((WIN * SLOTS, LANES), BF), S((C, 128), F32), S((C, 128), F32),
        S((3 * C, C), BF), S((C, C), BF), S((HID, C), BF), S((HID, C), BF), S((16, C), BF), S((C, 16), BF),
    ]
    return pl.pallas_call(ready_kernel, out_shape=out, in_specs=[VMEM] * 9, out_specs=[VMEM] * 10, compiler_params=SMALL)(
        region, labels, attn_gain.reshape(1, C), mlp_gain.reshape(1, C),
        qkv_weight, proj_weight, up_weight, down_weight, head_weight,
    )


def gradient(pieces, prepared, weights, scale):
    ids, sel, gain1, gain2, qkv_t, proj_t, up_t, down, head_t, head = prepared
    qkv_weight, proj_weight, up_weight, down_t = weights
    return pl.pallas_call(
        functools.partial(main_kernel, scale),
        out_shape=[PIECE] * 4,
        in_specs=[VMEM] * 18,
        out_specs=[VMEM] * 4,
        scratch_shapes=[
            pltpu.VMEM((WINDOWS, C, LANES), F32),
            pltpu.VMEM((WINDOWS, C, LANES), BF),
            pltpu.VMEM((HEADS, LANES, LANES), BF),
            pltpu.VMEM((HID, LANES), F32),
            pltpu.VMEM((16, LANES), F32),
        ],
        compiler_params=pltpu.CompilerParams(vmem_limit_bytes=32 * 2**20),
    )(
        *pieces, ids, sel, gain1, gain2, qkv_weight, qkv_t, proj_weight, proj_t,
        up_weight, up_t, down, down_t, head, head_t,
    )


def moved(piece, axes, steps):
    sizes = [lax.axis_size(a) for a in axes]
    route = []
    if len(axes) == 1:
        (n,) = sizes
        route = [((i - steps) % n, i) for i in range(n)]
    else:
        n, m = sizes
        for i in range(n):
            for j in range(m):
                route.append((((i - steps) % n) * m + (j - steps) % m, i * m + j))
    return lax.ppermute(piece, axes if len(axes) > 1 else axes[0], route)


ROADS = (("gz",), ("gy",), ("gz", "gy"))


def body(
    features, region, labels, attn_gain, qkv_weight, proj_weight, mlp_gain, up_weight, down_weight, head_weight,
):
    own, *away = cut(features)
    down_t = down_weight.T
    arrived = [moved(piece, road, -1) for piece, road in zip(away, ROADS)]
    prepared = ready(
        region, labels, attn_gain, mlp_gain, qkv_weight, proj_weight, up_weight, down_t, head_weight.T
    )
    scale = 1.0 / (WIN * WIN * NX * lax.axis_size("gz") * lax.axis_size("gy"))
    own, *away = gradient((own, *arrived), prepared, (qkv_weight, proj_weight, up_weight, down_t), scale)
    arrived = [moved(piece, road, 1) for piece, road in zip(away, ROADS)]
    return join(own, *arrived)


def solution(mesh):
    cells = P("gz", "gy", None)
    in_specs = (cells, cells, cells) + (P(),) * 7
    return jax.shard_map(body, mesh=mesh, in_specs=in_specs, out_specs=cells, check_vma=False)
```

```python
import functools

import jax
import jax.numpy as jnp
from jax import lax
from jax.experimental import pallas as pl
from jax.experimental.pallas import tpu as pltpu
from jax.sharding import PartitionSpec as P

C = 96
HEADS = 6
HEAD = 16
HID = 384
CLASSES = 14
WIN = 7
SHIFT = 3
KEEP = WIN - SHIFT
NX = 28
WINDOWS = 4
TOKENS = 343
LANES = 384
ROWS = 352
PAIRS = 3
SLOTS = 64
WIDE = NX * C
FAR = -(2.0**30)
LOG2E = 1.4426950408889634
LN2 = 0.6931471805599453
BF = jnp.bfloat16
F32 = jnp.float32


def nn(a, b):
    return lax.dot_general(a, b, (((1,), (0,)), ((), ())), preferred_element_type=F32)


def nt(a, b):
    return lax.dot_general(a, b, (((1,), (1,)), ((), ())), preferred_element_type=F32)


def piece_rows(cells, depths, rows):
    parts = [cells[d][rows[0] : rows[1]] for d in depths]
    used = len(depths) * (rows[1] - rows[0])
    if used < 16:
        parts.append(jnp.zeros((16 - used, parts[0].shape[1]), parts[0].dtype))
    return jnp.concatenate(parts, axis=0)


def cut_kernel(f_ref, a_ref, b_ref, c_ref, d_ref):
    cells = [f_ref[d].astype(F32) for d in range(WIN)]
    low, high = range(SHIFT), range(SHIFT, WIN)
    a_ref[...] = piece_rows(cells, high, (SHIFT, WIN)).astype(BF)
    b_ref[...] = piece_rows(cells, low, (SHIFT, WIN)).astype(BF)
    c_ref[...] = piece_rows(cells, high, (0, SHIFT)).astype(BF)
    d_ref[...] = piece_rows(cells, low, (0, SHIFT)).astype(BF)


def join_kernel(a_ref, b_ref, c_ref, d_ref, out_ref):
    a = a_ref[...].astype(F32)
    b = b_ref[...].astype(F32)
    c = c_ref[...].astype(F32)
    d = d_ref[...].astype(F32)
    for i in range(WIN):
        if i < SHIFT:
            left, right, k = d, b, i
        else:
            left, right, k = c, a, i - SHIFT
        rows = [left[SHIFT * k : SHIFT * k + SHIFT], right[KEEP * k : KEEP * k + KEEP]]
        out_ref[i] = jnp.concatenate(rows, axis=0).astype(BF)


def selector():
    token = lax.broadcasted_iota(jnp.int32, (1, LANES), 1)
    column = (token * 1338) >> 16
    cell = token - 49 * column
    slot = 64 * column + cell + 4 * (cell >= 28).astype(jnp.int32) + 4 * (cell >= 40).astype(jnp.int32)
    slot = jnp.where(token < TOKENS, slot, -1)
    place = lax.broadcasted_iota(jnp.int32, (WIN * SLOTS, LANES), 0)
    return (place == slot).astype(F32).astype(BF)


def by_slots(values):
    cells = [values[d] for d in range(WIN)]
    low, high = range(KEEP), range(KEEP, WIN)
    return jnp.concatenate(
        [
            piece_rows(cells, low, (0, KEEP)),
            piece_rows(cells, high, (0, KEEP)),
            piece_rows(cells, low, (KEEP, WIN)),
            piece_rows(cells, high, (KEEP, WIN)),
        ],
        axis=0,
    )


def turned(values):
    return values.astype(F32).T.astype(BF)


def ready_kernel(
    region_ref, labels_ref, g1_ref, g2_ref, qkv_ref, proj_ref, up_ref, downt_ref, head_ref,
    ids_ref, sel_ref, gain1_ref, gain2_ref, qkvt_ref, projt_ref, upt_ref, down_ref, headt_ref, heads_ref,
):
    sel = selector()
    sel_ref[...] = sel
    rows = []
    for ref in (region_ref, labels_ref):
        flat = by_slots(ref[...].astype(F32)).T
        for w in range(WINDOWS):
            rows.append(jnp.concatenate([flat[WIN * w + c : WIN * w + c + 1] for c in range(WIN)], axis=1))
    ids = nn(jnp.concatenate(rows, axis=0).astype(BF), sel)
    token = lax.broadcasted_iota(jnp.int32, ids.shape, 1)
    row = lax.broadcasted_iota(jnp.int32, ids.shape, 0)
    ids_ref[...] = jnp.where(token < TOKENS, ids, jnp.where(row < WINDOWS, 4.0, -1.0))
    for ref, out in ((g1_ref, gain1_ref), (g2_ref, gain2_ref)):
        out[...] = jnp.broadcast_to(ref[...], (128, C)).T
    qkvt_ref[...] = turned(qkv_ref[...])
    projt_ref[...] = turned(proj_ref[...])
    upt_ref[...] = turned(up_ref[...])
    down_ref[...] = turned(downt_ref[...])
    head = jnp.concatenate([head_ref[...].astype(F32), jnp.zeros((2, C), F32)], axis=0)
    headt_ref[...] = head.astype(BF)
    heads_ref[...] = head.T.astype(BF)


def norm(values, gain):
    center = values - jnp.mean(values, axis=0, keepdims=True)
    inverse = lax.rsqrt(jnp.mean(center * center, axis=0, keepdims=True) + 1e-5)
    unit = center * inverse
    return unit, inverse, (unit * gain).astype(BF)


def norm_back(cotangent, unit, inverse, gain):
    scaled = cotangent * gain
    middle = jnp.mean(scaled, axis=0, keepdims=True)
    along = jnp.mean(scaled * unit, axis=0, keepdims=True)
    return inverse * (scaled - middle - unit * along)


def paired(pair, rows, extra, second=None):
    halves = []
    for h in range(2):
        head = 2 * pair + h
        parts = [rows[HEAD * h : HEAD * h + HEAD], extra if h == 0 or second is None else second, jnp.zeros((16, LANES), BF)]
        if head < HEADS - 1:
            parts.insert(1, jnp.zeros((C - HEAD * head - HEAD, LANES), BF))
        if head:
            parts.insert(0, jnp.zeros((HEAD * head, LANES), BF))
        halves.append(jnp.concatenate(parts, axis=0))
    return jnp.concatenate(halves, axis=1)


def blockdiag(rows):
    blank = jnp.zeros((HEAD, LANES), BF)
    first = jnp.concatenate([rows[:HEAD], blank], axis=1)
    second = jnp.concatenate([blank, rows[HEAD:]], axis=1)
    return jnp.concatenate([first, second], axis=0)


def across(ref):
    return jnp.concatenate([ref[w] for w in range(WINDOWS)], axis=1)


def split(ref, values):
    for w in range(WINDOWS):
        ref[w] = values[:, LANES * w : LANES * w + LANES]


def main_kernel(
    scale,
    a_ref, b_ref, c_ref, d_ref, ids_ref, sel_ref, gain1_ref, gain2_ref,
    qkv_ref, qkvt_ref, proj_ref, projt_ref, up_ref, upt_ref, down_ref, downt_ref, head_ref, headt_ref,
    oa_ref, ob_ref, oc_ref, od_ref,
    x_ref, mixed_qkv_ref, keyst_ref, valuest_ref, side_ref, e_ref, ds_ref, attended_ref, inverse_ref,
    d_hidden_ref, d_mixed_ref, extra_ref, d_qkv_ref, slope_ref,
):
    sel = sel_ref[...]
    rows = jnp.concatenate([r[...].astype(F32) for r in (a_ref, b_ref, c_ref, d_ref)], axis=0)
    tall = rows.T
    for w in range(WINDOWS):
        cols = [(WIN * w + SHIFT + c) % NX for c in range(WIN)]
        wide = jnp.concatenate([tall[C * c : C * c + C] for c in cols], axis=1).astype(BF)
        x_ref[:, LANES * w : LANES * w + LANES] = nn(wide, sel)
    e_ref[:, :, ROWS:, :] = jnp.zeros((WINDOWS, PAIRS, LANES - ROWS, 2 * LANES), BF)
    ds_ref[:, ROWS:, :] = jnp.zeros((PAIRS, LANES - ROWS, 2 * LANES), BF)

    gain1 = jnp.concatenate([gain1_ref[...]] * (3 * WINDOWS), axis=1)
    gain2 = jnp.concatenate([gain2_ref[...]] * (3 * WINDOWS), axis=1)
    unit1, inverse1, normed1 = norm(x_ref[...], gain1)
    for k in range(3):
        part = nn(qkvt_ref[C * k : C * k + C, :], normed1)
        part = (part * (0.25 * LOG2E) if k == 0 else part).astype(BF)
        for w in range(WINDOWS):
            mixed_qkv_ref[w, C * k : C * k + C, :] = part[:, LANES * w : LANES * w + LANES]
    index = lax.broadcasted_iota(jnp.int32, (16, LANES), 0)
    ones = jnp.where(index < 2, 1.0, 0.0).astype(BF)
    blank = jnp.zeros((16, LANES), BF)
    for w in range(WINDOWS):
        same = index.astype(F32) == ids_ref[w : w + 1, :]
        key_side = same.astype(F32).astype(BF)
        side_ref[w] = jnp.where(same | (index > 4), 0.0, FAR).astype(BF)
        keyst_ref[w] = turned(jnp.concatenate([mixed_qkv_ref[w, C : 2 * C, :], key_side, blank], axis=0))[:ROWS]
        valuest_ref[w] = turned(jnp.concatenate([mixed_qkv_ref[w, 2 * C :, :], ones, blank], axis=0))[:ROWS]

    units = [(p, j) for p in range(PAIRS) for j in range(3)]

    def forward(w, carry):
        keys_t = keyst_ref[w]
        side = side_ref[w]
        spread = [paired(p, mixed_qkv_ref[w, 32 * p : 32 * p + 32, :], side) for p in range(PAIRS)]
        scores_of = lambda p, j: nn(keys_t, spread[p][:, 256 * j : 256 * j + 256])
        following = scores_of(*units[0])
        mixed = []
        for u, (p, j) in enumerate(units):
            scores = following
            if u + 1 < len(units):
                following = scores_of(*units[u + 1])
            top = jnp.max(scores, axis=0, keepdims=True)
            raised = jnp.exp2(scores - top).astype(BF)
            e_ref[w, p, :ROWS, 256 * j : 256 * j + 256] = raised
            values = mixed_qkv_ref[w, 2 * C + 32 * p : 2 * C + 32 * p + 32, :]
            mixed.append(nn(jnp.concatenate([values, ones], axis=0)[:, :ROWS], raised))
            if j == 2:
                whole = jnp.concatenate(mixed, axis=1)
                mixed = []
                inverse_sum = 1.0 / whole[32:33]
                for h in range(2):
                    inverse_head = inverse_sum[:, LANES * h : LANES * h + LANES]
                    inverse_ref[w, 2 * p + h : 2 * p + h + 1, :] = inverse_head
                    own = whole[HEAD * h : HEAD * h + HEAD, LANES * h : LANES * h + LANES]
                    place = 32 * p + HEAD * h
                    attended_ref[w, place : place + HEAD, :] = (own * inverse_head).astype(BF)
        return carry

    lax.fori_loop(0, WINDOWS, forward, 0)

    attended = across(attended_ref)
    hidden = x_ref[...] + nn(projt_ref[...], attended)
    unit2, inverse2, normed2 = norm(hidden, gain2)
    output = hidden
    for j in range(3):
        part = slice(128 * j, 128 * j + 128)
        raised = nn(upt_ref[part, :], normed2)
        below = 0.5 + 0.5 * lax.erf(raised * (0.5**0.5))
        bell = jnp.exp(-0.5 * raised * raised) * 0.3989422804014327
        slope_ref[part, :] = below + raised * bell
        output = output + nn(downt_ref[:, part], (raised * below).astype(BF))
    logits = nn(headt_ref[...], output.astype(BF))
    labels = jnp.concatenate([ids_ref[WINDOWS + w : WINDOWS + w + 1, :] for w in range(WINDOWS)], axis=1)
    kind = lax.broadcasted_iota(jnp.int32, (16, WINDOWS * LANES), 0)
    logits = jnp.where(kind < CLASSES, logits, -1e30)
    powers = jnp.exp(logits - jnp.max(logits, axis=0, keepdims=True))
    soft = powers / jnp.sum(powers, axis=0, keepdims=True)
    at_label = (kind.astype(F32) == labels).astype(F32)
    d_logits = jnp.where(labels >= 0.0, (soft - at_label) * scale, 0.0)
    d_output = nn(head_ref[...], d_logits.astype(BF)).astype(BF)
    d_normed2 = jnp.zeros((C, WINDOWS * LANES), F32)
    for j in range(3):
        part = slice(128 * j, 128 * j + 128)
        d_expanded = nn(down_ref[part, :], d_output)
        d_raised = (d_expanded * slope_ref[part, :]).astype(BF)
        d_normed2 = d_normed2 + nn(up_ref[:, part], d_raised)
    d_hidden = d_output.astype(F32) + norm_back(d_normed2, unit2, inverse2, gain2)
    d_hidden_ref[...] = d_hidden
    d_attended = nn(proj_ref[...], d_hidden.astype(BF))
    for h in range(HEADS):
        own = slice(HEAD * h, HEAD * h + HEAD)
        sums = jnp.concatenate([inverse_ref[w, h : h + 1, :] for w in range(WINDOWS)], axis=1)
        d_mixed = (d_attended[own] * sums).astype(BF)
        along = -jnp.sum(d_mixed.astype(F32) * attended[own].astype(F32), axis=0, keepdims=True)
        coarse = along.astype(BF).astype(F32)
        rest = along - coarse
        for w in range(WINDOWS):
            lanes = slice(LANES * w, LANES * w + LANES)
            d_mixed_ref[w, own, :] = d_mixed[:, lanes]
            extra = jnp.where(index == 0, coarse[:, lanes], jnp.where(index == 1, rest[:, lanes], 0.0))
            extra_ref[w, own, :] = extra.astype(BF)

    def backward(w, carry):
        values_t = valuest_ref[w]
        spread = [
            paired(p, d_mixed_ref[w, 32 * p : 32 * p + 32, :], *[extra_ref[w, 32 * p + HEAD * h : 32 * p + HEAD * h + HEAD, :] for h in range(2)])
            for p in range(PAIRS)
        ]
        weights_of = lambda p, j: nn(values_t, spread[p][:, 256 * j : 256 * j + 256])
        following = weights_of(*units[0])
        both = []
        for u, (p, j) in enumerate(units):
            own = slice(32 * p, 32 * p + 32)
            cols = slice(256 * j, 256 * j + 256)
            d_weights = following
            if u + 1 < len(units):
                following = weights_of(*units[u + 1])
            d_scores = (e_ref[w, p, :ROWS, cols].astype(F32) * d_weights).astype(BF)
            ds_ref[p, :ROWS, cols] = d_scores
            keys = mixed_qkv_ref[w, C + 32 * p : C + 32 * p + 32, :]
            both.append(nn(keys[:, :ROWS], d_scores))
            if j == 2:
                whole = jnp.concatenate(both, axis=1) * 0.25
                both = []
                d_queries = jnp.concatenate([whole[:HEAD, :LANES], whole[HEAD:, LANES:]], axis=0)
                d_qkv_ref[w, own, :] = d_queries.astype(BF)
                d_keys = nt(blockdiag(mixed_qkv_ref[w, own, :]), ds_ref[p]) * LN2
                d_qkv_ref[w, C + 32 * p : C + 32 * p + 32, :] = d_keys.astype(BF)
                d_values = nt(blockdiag(d_mixed_ref[w, own, :]), e_ref[w, p])
                d_qkv_ref[w, 2 * C + 32 * p : 2 * C + 32 * p + 32, :] = d_values.astype(BF)
        return carry

    lax.fori_loop(0, WINDOWS, backward, 0)

    d_normed1 = nn(qkv_ref[...], across(d_qkv_ref))
    unit1, inverse1, normed1 = norm(x_ref[...], gain1)
    grad = (d_hidden_ref[...] + norm_back(d_normed1, unit1, inverse1, gain1)).astype(BF)
    blocks = [None] * NX
    for w in range(WINDOWS):
        wide = nt(grad[:, LANES * w : LANES * w + LANES], sel)
        for c in range(WIN):
            blocks[(WIN * w + SHIFT + c) % NX] = wide[:, SLOTS * c : SLOTS * c + SLOTS]
    rows = jnp.concatenate(blocks, axis=0).T
    for k, ref in enumerate((oa_ref, ob_ref, oc_ref, od_ref)):
        ref[...] = rows[16 * k : 16 * k + 16].astype(BF)


VMEM = pl.BlockSpec(memory_space=pltpu.VMEM)
SMALL = pltpu.CompilerParams(vmem_limit_bytes=8 * 2**20)
PIECE = jax.ShapeDtypeStruct((16, WIDE), BF)


def cut(features):
    return pl.pallas_call(cut_kernel, out_shape=[PIECE] * 4, in_specs=[VMEM], out_specs=[VMEM] * 4, compiler_params=SMALL)(features)


def join(*pieces):
    out = jax.ShapeDtypeStruct((WIN, WIN, WIDE), BF)
    return pl.pallas_call(join_kernel, out_shape=out, in_specs=[VMEM] * 4, out_specs=VMEM, compiler_params=SMALL)(*pieces)


def ready(region, labels, attn_gain, mlp_gain, qkv_weight, proj_weight, up_weight, down_weight, head_weight):
    S = jax.ShapeDtypeStruct
    out = [
        S((8, LANES), F32), S((WIN * SLOTS, LANES), BF), S((C, 128), F32), S((C, 128), F32),
        S((3 * C, C), BF), S((C, C), BF), S((HID, C), BF), S((HID, C), BF), S((16, C), BF), S((C, 16), BF),
    ]
    return pl.pallas_call(ready_kernel, out_shape=out, in_specs=[VMEM] * 9, out_specs=[VMEM] * 10, compiler_params=SMALL)(
        region, labels, attn_gain.reshape(1, C), mlp_gain.reshape(1, C),
        qkv_weight, proj_weight, up_weight, down_weight, head_weight,
    )


def gradient(pieces, prepared, weights, scale):
    ids, sel, gain1, gain2, qkv_t, proj_t, up_t, down, head_t, head = prepared
    qkv_weight, proj_weight, up_weight, down_t = weights
    return pl.pallas_call(
        functools.partial(main_kernel, scale),
        out_shape=[PIECE] * 4,
        in_specs=[VMEM] * 18,
        out_specs=[VMEM] * 4,
        scratch_shapes=[
            pltpu.VMEM((C, WINDOWS * LANES), F32),
            pltpu.VMEM((WINDOWS, 3 * C, LANES), BF),
            pltpu.VMEM((WINDOWS, ROWS, 128), BF),
            pltpu.VMEM((WINDOWS, ROWS, 128), BF),
            pltpu.VMEM((WINDOWS, 16, LANES), BF),
            pltpu.VMEM((WINDOWS, PAIRS, LANES, 2 * LANES), BF),
            pltpu.VMEM((PAIRS, LANES, 2 * LANES), BF),
            pltpu.VMEM((WINDOWS, C, LANES), BF),
            pltpu.VMEM((WINDOWS, 8, LANES), F32),
            pltpu.VMEM((C, WINDOWS * LANES), F32),
            pltpu.VMEM((WINDOWS, C, LANES), BF),
            pltpu.VMEM((WINDOWS, C, LANES), BF),
            pltpu.VMEM((WINDOWS, 3 * C, LANES), BF),
            pltpu.VMEM((HID, WINDOWS * LANES), F32),
        ],
        compiler_params=pltpu.CompilerParams(vmem_limit_bytes=32 * 2**20),
    )(
        *pieces, ids, sel, gain1, gain2, qkv_weight, qkv_t, proj_weight, proj_t,
        up_weight, up_t, down, down_t, head, head_t,
    )


def moved(piece, axes, steps):
    sizes = [lax.axis_size(a) for a in axes]
    route = []
    if len(axes) == 1:
        (n,) = sizes
        route = [((i - steps) % n, i) for i in range(n)]
    else:
        n, m = sizes
        for i in range(n):
            for j in range(m):
                route.append((((i - steps) % n) * m + (j - steps) % m, i * m + j))
    return lax.ppermute(piece, axes if len(axes) > 1 else axes[0], route)


ROADS = (("gz",), ("gy",), ("gz", "gy"))


def body(
    features, region, labels, attn_gain, qkv_weight, proj_weight, mlp_gain, up_weight, down_weight, head_weight,
):
    own, *away = cut(features)
    down_t = down_weight.T
    arrived = [moved(piece, road, -1) for piece, road in zip(away, ROADS)]
    prepared = ready(
        region, labels, attn_gain, mlp_gain, qkv_weight, proj_weight, up_weight, down_t, head_weight.T
    )
    scale = 1.0 / (WIN * WIN * NX * lax.axis_size("gz") * lax.axis_size("gy"))
    own, *away = gradient((own, *arrived), prepared, (qkv_weight, proj_weight, up_weight, down_t), scale)
    arrived = [moved(piece, road, 1) for piece, road in zip(away, ROADS)]
    return join(own, *arrived)


def solution(mesh):
    cells = P("gz", "gy", None)
    in_specs = (cells, cells, cells) + (P(),) * 7
    return jax.shard_map(body, mesh=mesh, in_specs=in_specs, out_specs=cells, check_vma=False)
```

```python
import functools

import jax
import jax.numpy as jnp
from jax import lax
from jax.experimental import pallas as pl
from jax.experimental.pallas import tpu as pltpu
from jax.sharding import PartitionSpec as P

C = 96
HEADS = 6
HEAD = 16
HID = 384
CLASSES = 14
WIN = 7
SHIFT = 3
KEEP = WIN - SHIFT
NX = 28
WINDOWS = 4
TOKENS = 343
LANES = 384
ROWS = 352
PAIRS = 3
SLOTS = 64
WIDE = NX * C
HALF = 1408
FAR = -(2.0**30)
LOG2E = 1.4426950408889634
LN2 = 0.6931471805599453
BF = jnp.bfloat16
F32 = jnp.float32


def nn(a, b):
    return lax.dot_general(a, b, (((1,), (0,)), ((), ())), preferred_element_type=F32)


def nt(a, b):
    return lax.dot_general(a, b, (((1,), (1,)), ((), ())), preferred_element_type=F32)


def piece_rows(cells, depths, rows):
    parts = [cells[d][rows[0] : rows[1]] for d in depths]
    used = len(depths) * (rows[1] - rows[0])
    if used < 16:
        parts.append(jnp.zeros((16 - used, parts[0].shape[1]), parts[0].dtype))
    return jnp.concatenate(parts, axis=0)


def packed(rows, count):
    if count == 12:
        rest = rows[8:12]
        last = jnp.concatenate([rest[:, HALF:], jnp.zeros((4, 2 * HALF - WIDE), F32)], axis=1)
        tail = jnp.concatenate([rest[:, :HALF], last], axis=0)
    else:
        parts = [rows[8:9, LANES * k : LANES * k + LANES] for k in range(WIN)]
        tail = jnp.concatenate(parts + [jnp.zeros((1, LANES), F32)], axis=0)
    return jnp.concatenate([rows[:8], tail], axis=1).astype(BF)


def unpacked(ref, count):
    values = ref[...].astype(F32)
    tail = values[:, WIDE:]
    if count == 12:
        rest = jnp.concatenate([tail[:4], tail[4:8, : WIDE - HALF]], axis=1)
    else:
        rest = jnp.concatenate([tail[k : k + 1] for k in range(WIN)], axis=1)
    blank = jnp.zeros((16 - count, WIDE), F32)
    return jnp.concatenate([values[:, :WIDE], rest, blank], axis=0)


def cut_kernel(f_ref, a_ref, b_ref, c_ref, d_ref):
    cells = [f_ref[d].astype(F32) for d in range(WIN)]
    low, high = range(SHIFT), range(SHIFT, WIN)
    a_ref[...] = piece_rows(cells, high, (SHIFT, WIN)).astype(BF)
    b_ref[...] = packed(piece_rows(cells, low, (SHIFT, WIN)), 12)
    c_ref[...] = packed(piece_rows(cells, high, (0, SHIFT)), 12)
    d_ref[...] = packed(piece_rows(cells, low, (0, SHIFT)), 9)


def join_kernel(a_ref, b_ref, c_ref, d_ref, out_ref):
    a = a_ref[...].astype(F32)
    b = unpacked(b_ref, 12)
    c = unpacked(c_ref, 12)
    d = unpacked(d_ref, 9)
    for i in range(WIN):
        if i < SHIFT:
            left, right, k = d, b, i
        else:
            left, right, k = c, a, i - SHIFT
        rows = [left[SHIFT * k : SHIFT * k + SHIFT], right[KEEP * k : KEEP * k + KEEP]]
        out_ref[i] = jnp.concatenate(rows, axis=0).astype(BF)


def selector():
    token = lax.broadcasted_iota(jnp.int32, (1, LANES), 1)
    column = (token * 1338) >> 16
    cell = token - 49 * column
    slot = 64 * column + cell + 4 * (cell >= 28).astype(jnp.int32) + 4 * (cell >= 40).astype(jnp.int32)
    slot = jnp.where(token < TOKENS, slot, -1)
    place = lax.broadcasted_iota(jnp.int32, (WIN * SLOTS, LANES), 0)
    return (place == slot).astype(F32).astype(BF)


def by_slots(values):
    cells = [values[d] for d in range(WIN)]
    low, high = range(KEEP), range(KEEP, WIN)
    return jnp.concatenate(
        [
            piece_rows(cells, low, (0, KEEP)),
            piece_rows(cells, high, (0, KEEP)),
            piece_rows(cells, low, (KEEP, WIN)),
            piece_rows(cells, high, (KEEP, WIN)),
        ],
        axis=0,
    )


def turned(values):
    return values.astype(F32).T.astype(BF)


def ready_kernel(
    region_ref, labels_ref, g1_ref, g2_ref, qkv_ref, proj_ref, up_ref, downt_ref, head_ref,
    ids_ref, sel_ref, gain1_ref, gain2_ref, qkvt_ref, projt_ref, upt_ref, down_ref, headt_ref, heads_ref,
):
    sel = selector()
    sel_ref[...] = sel
    rows = []
    for ref in (region_ref, labels_ref):
        flat = by_slots(ref[...].astype(F32)).T
        for w in range(WINDOWS):
            rows.append(jnp.concatenate([flat[WIN * w + c : WIN * w + c + 1] for c in range(WIN)], axis=1))
    ids = nn(jnp.concatenate(rows, axis=0).astype(BF), sel)
    token = lax.broadcasted_iota(jnp.int32, ids.shape, 1)
    row = lax.broadcasted_iota(jnp.int32, ids.shape, 0)
    ids_ref[...] = jnp.where(token < TOKENS, ids, jnp.where(row < WINDOWS, 4.0, -1.0))
    for ref, out in ((g1_ref, gain1_ref), (g2_ref, gain2_ref)):
        out[...] = jnp.broadcast_to(ref[...], (128, C)).T
    qkvt_ref[...] = turned(qkv_ref[...])
    projt_ref[...] = turned(proj_ref[...])
    upt_ref[...] = turned(up_ref[...])
    down_ref[...] = turned(downt_ref[...])
    head = jnp.concatenate([head_ref[...].astype(F32), jnp.zeros((2, C), F32)], axis=0)
    headt_ref[...] = head.astype(BF)
    heads_ref[...] = head.T.astype(BF)


def norm(values, gain):
    center = values - jnp.mean(values, axis=0, keepdims=True)
    inverse = lax.rsqrt(jnp.mean(center * center, axis=0, keepdims=True) + 1e-5)
    unit = center * inverse
    return unit, inverse, (unit * gain).astype(BF)


def norm_back(cotangent, unit, inverse, gain):
    scaled = cotangent * gain
    middle = jnp.mean(scaled, axis=0, keepdims=True)
    along = jnp.mean(scaled * unit, axis=0, keepdims=True)
    return inverse * (scaled - middle - unit * along)


def paired(pair, rows, extra, second=None):
    halves = []
    for h in range(2):
        head = 2 * pair + h
        parts = [rows[HEAD * h : HEAD * h + HEAD], extra if h == 0 or second is None else second, jnp.zeros((16, LANES), BF)]
        if head < HEADS - 1:
            parts.insert(1, jnp.zeros((C - HEAD * head - HEAD, LANES), BF))
        if head:
            parts.insert(0, jnp.zeros((HEAD * head, LANES), BF))
        halves.append(jnp.concatenate(parts, axis=0))
    return jnp.concatenate(halves, axis=1)


def blockdiag(rows):
    blank = jnp.zeros((HEAD, LANES), BF)
    first = jnp.concatenate([rows[:HEAD], blank], axis=1)
    second = jnp.concatenate([blank, rows[HEAD:]], axis=1)
    return jnp.concatenate([first, second], axis=0)


def across(ref):
    return jnp.concatenate([ref[w] for w in range(WINDOWS)], axis=1)


def split(ref, values):
    for w in range(WINDOWS):
        ref[w] = values[:, LANES * w : LANES * w + LANES]


def main_kernel(
    scale,
    a_ref, b_ref, c_ref, d_ref, ids_ref, sel_ref, gain1_ref, gain2_ref,
    qkv_ref, qkvt_ref, proj_ref, projt_ref, up_ref, upt_ref, down_ref, downt_ref, head_ref, headt_ref,
    oa_ref, ob_ref, oc_ref, od_ref,
    x_ref, mixed_qkv_ref, keyst_ref, valuest_ref, side_ref, e_ref, ds_ref, attended_ref, inverse_ref,
    d_hidden_ref, d_mixed_ref, extra_ref, d_qkv_ref, slope_ref,
):
    sel = sel_ref[...]
    pieces = [a_ref[...].astype(F32), unpacked(b_ref, 12), unpacked(c_ref, 12), unpacked(d_ref, 9)]
    rows = jnp.concatenate(pieces, axis=0)
    tall = rows.T
    for w in range(WINDOWS):
        cols = [(WIN * w + SHIFT + c) % NX for c in range(WIN)]
        wide = jnp.concatenate([tall[C * c : C * c + C] for c in cols], axis=1).astype(BF)
        x_ref[:, LANES * w : LANES * w + LANES] = nn(wide, sel)
    e_ref[:, :, ROWS:, :] = jnp.zeros((WINDOWS, PAIRS, LANES - ROWS, 2 * LANES), BF)
    ds_ref[:, ROWS:, :] = jnp.zeros((PAIRS, LANES - ROWS, 2 * LANES), BF)

    gain1 = jnp.concatenate([gain1_ref[...]] * (3 * WINDOWS), axis=1)
    gain2 = jnp.concatenate([gain2_ref[...]] * (3 * WINDOWS), axis=1)
    unit1, inverse1, normed1 = norm(x_ref[...], gain1)
    for k in range(3):
        part = nn(qkvt_ref[C * k : C * k + C, :], normed1)
        part = (part * (0.25 * LOG2E) if k == 0 else part).astype(BF)
        for w in range(WINDOWS):
            mixed_qkv_ref[w, C * k : C * k + C, :] = part[:, LANES * w : LANES * w + LANES]
    index = lax.broadcasted_iota(jnp.int32, (16, LANES), 0)
    ones = jnp.where(index < 2, 1.0, 0.0).astype(BF)
    blank = jnp.zeros((16, LANES), BF)
    for w in range(WINDOWS):
        same = index.astype(F32) == ids_ref[w : w + 1, :]
        key_side = same.astype(F32).astype(BF)
        side_ref[w] = jnp.where(same | (index > 4), 0.0, FAR).astype(BF)
        keyst_ref[w] = turned(jnp.concatenate([mixed_qkv_ref[w, C : 2 * C, :], key_side, blank], axis=0))[:ROWS]
        valuest_ref[w] = turned(jnp.concatenate([mixed_qkv_ref[w, 2 * C :, :], ones, blank], axis=0))[:ROWS]

    units = [(p, j) for p in range(PAIRS) for j in range(3)]

    def forward(w, carry):
        keys_t = keyst_ref[w]
        side = side_ref[w]
        spread = [paired(p, mixed_qkv_ref[w, 32 * p : 32 * p + 32, :], side) for p in range(PAIRS)]
        scores_of = lambda p, j: nn(keys_t, spread[p][:, 256 * j : 256 * j + 256])
        following = scores_of(*units[0])
        mixed = []
        for u, (p, j) in enumerate(units):
            scores = following
            if u + 1 < len(units):
                following = scores_of(*units[u + 1])
            top = jnp.max(scores, axis=0, keepdims=True)
            raised = jnp.exp2(scores - top).astype(BF)
            e_ref[w, p, :ROWS, 256 * j : 256 * j + 256] = raised
            values = mixed_qkv_ref[w, 2 * C + 32 * p : 2 * C + 32 * p + 32, :]
            mixed.append(nn(jnp.concatenate([values, ones], axis=0)[:, :ROWS], raised))
            if j == 2:
                whole = jnp.concatenate(mixed, axis=1)
                mixed = []
                inverse_sum = 1.0 / whole[32:33]
                for h in range(2):
                    inverse_head = inverse_sum[:, LANES * h : LANES * h + LANES]
                    inverse_ref[w, 2 * p + h : 2 * p + h + 1, :] = inverse_head
                    own = whole[HEAD * h : HEAD * h + HEAD, LANES * h : LANES * h + LANES]
                    place = 32 * p + HEAD * h
                    attended_ref[w, place : place + HEAD, :] = (own * inverse_head).astype(BF)
        return carry

    lax.fori_loop(0, WINDOWS, forward, 0)

    attended = across(attended_ref)
    hidden = x_ref[...] + nn(projt_ref[...], attended)
    unit2, inverse2, normed2 = norm(hidden, gain2)
    output = hidden
    for j in range(3):
        part = slice(128 * j, 128 * j + 128)
        raised = nn(upt_ref[part, :], normed2)
        below = 0.5 + 0.5 * lax.erf(raised * (0.5**0.5))
        bell = jnp.exp(-0.5 * raised * raised) * 0.3989422804014327
        slope_ref[part, :] = below + raised * bell
        output = output + nn(downt_ref[:, part], (raised * below).astype(BF))
    logits = nn(headt_ref[...], output.astype(BF))
    labels = jnp.concatenate([ids_ref[WINDOWS + w : WINDOWS + w + 1, :] for w in range(WINDOWS)], axis=1)
    kind = lax.broadcasted_iota(jnp.int32, (16, WINDOWS * LANES), 0)
    logits = jnp.where(kind < CLASSES, logits, -1e30)
    powers = jnp.exp(logits - jnp.max(logits, axis=0, keepdims=True))
    soft = powers / jnp.sum(powers, axis=0, keepdims=True)
    at_label = (kind.astype(F32) == labels).astype(F32)
    d_logits = jnp.where(labels >= 0.0, (soft - at_label) * scale, 0.0)
    d_output = nn(head_ref[...], d_logits.astype(BF)).astype(BF)
    d_normed2 = jnp.zeros((C, WINDOWS * LANES), F32)
    for j in range(3):
        part = slice(128 * j, 128 * j + 128)
        d_expanded = nn(down_ref[part, :], d_output)
        d_raised = (d_expanded * slope_ref[part, :]).astype(BF)
        d_normed2 = d_normed2 + nn(up_ref[:, part], d_raised)
    d_hidden = d_output.astype(F32) + norm_back(d_normed2, unit2, inverse2, gain2)
    d_hidden_ref[...] = d_hidden
    d_attended = nn(proj_ref[...], d_hidden.astype(BF))
    for h in range(HEADS):
        own = slice(HEAD * h, HEAD * h + HEAD)
        sums = jnp.concatenate([inverse_ref[w, h : h + 1, :] for w in range(WINDOWS)], axis=1)
        d_mixed = (d_attended[own] * sums).astype(BF)
        along = -jnp.sum(d_mixed.astype(F32) * attended[own].astype(F32), axis=0, keepdims=True)
        coarse = along.astype(BF).astype(F32)
        rest = along - coarse
        for w in range(WINDOWS):
            lanes = slice(LANES * w, LANES * w + LANES)
            d_mixed_ref[w, own, :] = d_mixed[:, lanes]
            extra = jnp.where(index == 0, coarse[:, lanes], jnp.where(index == 1, rest[:, lanes], 0.0))
            extra_ref[w, own, :] = extra.astype(BF)

    def backward(w, carry):
        values_t = valuest_ref[w]
        spread = [
            paired(p, d_mixed_ref[w, 32 * p : 32 * p + 32, :], *[extra_ref[w, 32 * p + HEAD * h : 32 * p + HEAD * h + HEAD, :] for h in range(2)])
            for p in range(PAIRS)
        ]
        weights_of = lambda p, j: nn(values_t, spread[p][:, 256 * j : 256 * j + 256])
        following = weights_of(*units[0])
        both = []
        for u, (p, j) in enumerate(units):
            own = slice(32 * p, 32 * p + 32)
            cols = slice(256 * j, 256 * j + 256)
            d_weights = following
            if u + 1 < len(units):
                following = weights_of(*units[u + 1])
            d_scores = (e_ref[w, p, :ROWS, cols].astype(F32) * d_weights).astype(BF)
            ds_ref[p, :ROWS, cols] = d_scores
            keys = mixed_qkv_ref[w, C + 32 * p : C + 32 * p + 32, :]
            both.append(nn(keys[:, :ROWS], d_scores))
            if j == 2:
                whole = jnp.concatenate(both, axis=1) * 0.25
                both = []
                d_queries = jnp.concatenate([whole[:HEAD, :LANES], whole[HEAD:, LANES:]], axis=0)
                d_qkv_ref[w, own, :] = d_queries.astype(BF)
                d_keys = nt(blockdiag(mixed_qkv_ref[w, own, :]), ds_ref[p]) * LN2
                d_qkv_ref[w, C + 32 * p : C + 32 * p + 32, :] = d_keys.astype(BF)
                d_values = nt(blockdiag(d_mixed_ref[w, own, :]), e_ref[w, p])
                d_qkv_ref[w, 2 * C + 32 * p : 2 * C + 32 * p + 32, :] = d_values.astype(BF)
        return carry

    lax.fori_loop(0, WINDOWS, backward, 0)

    d_normed1 = nn(qkv_ref[...], across(d_qkv_ref))
    unit1, inverse1, normed1 = norm(x_ref[...], gain1)
    grad = (d_hidden_ref[...] + norm_back(d_normed1, unit1, inverse1, gain1)).astype(BF)
    blocks = [None] * NX
    for w in range(WINDOWS):
        wide = nt(grad[:, LANES * w : LANES * w + LANES], sel)
        for c in range(WIN):
            blocks[(WIN * w + SHIFT + c) % NX] = wide[:, SLOTS * c : SLOTS * c + SLOTS]
    rows = jnp.concatenate(blocks, axis=0).T
    oa_ref[...] = rows[:16].astype(BF)
    for k, (ref, count) in enumerate(((ob_ref, 12), (oc_ref, 12), (od_ref, 9))):
        ref[...] = packed(rows[16 * k + 16 : 16 * k + 32], count)


VMEM = pl.BlockSpec(memory_space=pltpu.VMEM)
SMALL = pltpu.CompilerParams(vmem_limit_bytes=8 * 2**20)
PIECES = [jax.ShapeDtypeStruct(s, BF) for s in ((16, WIDE), (8, 4096), (8, 4096), (8, 3072))]


def cut(features):
    return pl.pallas_call(cut_kernel, out_shape=PIECES, in_specs=[VMEM], out_specs=[VMEM] * 4, compiler_params=SMALL)(features)


def join(*pieces):
    out = jax.ShapeDtypeStruct((WIN, WIN, WIDE), BF)
    return pl.pallas_call(join_kernel, out_shape=out, in_specs=[VMEM] * 4, out_specs=VMEM, compiler_params=SMALL)(*pieces)


def ready(region, labels, attn_gain, mlp_gain, qkv_weight, proj_weight, up_weight, down_weight, head_weight):
    S = jax.ShapeDtypeStruct
    out = [
        S((8, LANES), F32), S((WIN * SLOTS, LANES), BF), S((C, 128), F32), S((C, 128), F32),
        S((3 * C, C), BF), S((C, C), BF), S((HID, C), BF), S((HID, C), BF), S((16, C), BF), S((C, 16), BF),
    ]
    return pl.pallas_call(ready_kernel, out_shape=out, in_specs=[VMEM] * 9, out_specs=[VMEM] * 10, compiler_params=SMALL)(
        region, labels, attn_gain.reshape(1, C), mlp_gain.reshape(1, C),
        qkv_weight, proj_weight, up_weight, down_weight, head_weight,
    )


def gradient(pieces, prepared, weights, scale):
    ids, sel, gain1, gain2, qkv_t, proj_t, up_t, down, head_t, head = prepared
    qkv_weight, proj_weight, up_weight, down_t = weights
    return pl.pallas_call(
        functools.partial(main_kernel, scale),
        out_shape=PIECES,
        in_specs=[VMEM] * 18,
        out_specs=[VMEM] * 4,
        scratch_shapes=[
            pltpu.VMEM((C, WINDOWS * LANES), F32),
            pltpu.VMEM((WINDOWS, 3 * C, LANES), BF),
            pltpu.VMEM((WINDOWS, ROWS, 128), BF),
            pltpu.VMEM((WINDOWS, ROWS, 128), BF),
            pltpu.VMEM((WINDOWS, 16, LANES), BF),
            pltpu.VMEM((WINDOWS, PAIRS, LANES, 2 * LANES), BF),
            pltpu.VMEM((PAIRS, LANES, 2 * LANES), BF),
            pltpu.VMEM((WINDOWS, C, LANES), BF),
            pltpu.VMEM((WINDOWS, 8, LANES), F32),
            pltpu.VMEM((C, WINDOWS * LANES), F32),
            pltpu.VMEM((WINDOWS, C, LANES), BF),
            pltpu.VMEM((WINDOWS, C, LANES), BF),
            pltpu.VMEM((WINDOWS, 3 * C, LANES), BF),
            pltpu.VMEM((HID, WINDOWS * LANES), F32),
        ],
        compiler_params=pltpu.CompilerParams(vmem_limit_bytes=32 * 2**20),
    )(
        *pieces, ids, sel, gain1, gain2, qkv_weight, qkv_t, proj_weight, proj_t,
        up_weight, up_t, down, down_t, head, head_t,
    )


def moved(piece, axes, steps):
    sizes = [lax.axis_size(a) for a in axes]
    route = []
    if len(axes) == 1:
        (n,) = sizes
        route = [((i - steps) % n, i) for i in range(n)]
    else:
        n, m = sizes
        for i in range(n):
            for j in range(m):
                route.append((((i - steps) % n) * m + (j - steps) % m, i * m + j))
    return lax.ppermute(piece, axes if len(axes) > 1 else axes[0], route)


ROADS = (("gz",), ("gy",), ("gz", "gy"))


def body(
    features, region, labels, attn_gain, qkv_weight, proj_weight, mlp_gain, up_weight, down_weight, head_weight,
):
    own, *away = cut(features)
    down_t = down_weight.T
    arrived = [moved(piece, road, -1) for piece, road in zip(away, ROADS)]
    prepared = ready(
        region, labels, attn_gain, mlp_gain, qkv_weight, proj_weight, up_weight, down_t, head_weight.T
    )
    scale = 1.0 / (WIN * WIN * NX * lax.axis_size("gz") * lax.axis_size("gy"))
    own, *away = gradient((own, *arrived), prepared, (qkv_weight, proj_weight, up_weight, down_t), scale)
    arrived = [moved(piece, road, 1) for piece, road in zip(away, ROADS)]
    return join(own, *arrived)


def solution(mesh):
    cells = P("gz", "gy", None)
    in_specs = (cells, cells, cells) + (P(),) * 7
    return jax.shard_map(body, mesh=mesh, in_specs=in_specs, out_specs=cells, check_vma=False)
```

```python
import functools

import jax
import jax.numpy as jnp
from jax import lax
from jax.experimental import pallas as pl
from jax.experimental.pallas import tpu as pltpu
from jax.sharding import PartitionSpec as P

C = 96
HEADS = 6
HEAD = 16
HID = 384
CLASSES = 14
WIN = 7
SHIFT = 3
KEEP = WIN - SHIFT
NX = 28
WINDOWS = 4
TOKENS = 343
LANES = 384
ROWS = 352
PAIRS = 3
SLOTS = 64
WIDE = NX * C
HALF = 1408
FAR = -(2.0**30)
LOG2E = 1.4426950408889634
LN2 = 0.6931471805599453
BF = jnp.bfloat16
F32 = jnp.float32


def nn(a, b):
    return lax.dot_general(a, b, (((1,), (0,)), ((), ())), preferred_element_type=F32)


def nt(a, b):
    return lax.dot_general(a, b, (((1,), (1,)), ((), ())), preferred_element_type=F32)


def piece_rows(cells, depths, rows):
    parts = [cells[d][rows[0] : rows[1]] for d in depths]
    used = len(depths) * (rows[1] - rows[0])
    if used < 16:
        parts.append(jnp.zeros((16 - used, parts[0].shape[1]), parts[0].dtype))
    return jnp.concatenate(parts, axis=0)


def packed(rows, count):
    if count == 12:
        rest = rows[8:12]
        last = jnp.concatenate([rest[:, HALF:], jnp.zeros((4, 2 * HALF - WIDE), F32)], axis=1)
        tail = jnp.concatenate([rest[:, :HALF], last], axis=0)
    else:
        parts = [rows[8:9, LANES * k : LANES * k + LANES] for k in range(WIN)]
        tail = jnp.concatenate(parts + [jnp.zeros((1, LANES), F32)], axis=0)
    return jnp.concatenate([rows[:8], tail], axis=1).astype(BF)


def unpacked(ref, count):
    values = ref[...].astype(F32)
    tail = values[:, WIDE:]
    if count == 12:
        rest = jnp.concatenate([tail[:4], tail[4:8, : WIDE - HALF]], axis=1)
    else:
        rest = jnp.concatenate([tail[k : k + 1] for k in range(WIN)], axis=1)
    blank = jnp.zeros((16 - count, WIDE), F32)
    return jnp.concatenate([values[:, :WIDE], rest, blank], axis=0)


def cut_kernel(f_ref, a_ref, c_ref, d_ref, b_ref):
    cells = [f_ref[d].astype(F32) for d in range(WIN)]
    low, high = range(SHIFT), range(SHIFT, WIN)
    a_ref[...] = piece_rows(cells, high, (SHIFT, WIN)).astype(BF)
    b_ref[...] = packed(piece_rows(cells, low, (SHIFT, WIN)), 12)
    c_ref[...] = packed(piece_rows(cells, high, (0, SHIFT)), 12)
    d_ref[...] = packed(piece_rows(cells, low, (0, SHIFT)), 9)


def join_kernel(a_ref, c_ref, d_ref, b_ref, out_ref):
    a = a_ref[...].astype(F32)
    b = unpacked(b_ref, 12)
    c = unpacked(c_ref, 12)
    d = unpacked(d_ref, 9)
    for i in range(WIN):
        if i < SHIFT:
            left, right, k = d, b, i
        else:
            left, right, k = c, a, i - SHIFT
        rows = [left[SHIFT * k : SHIFT * k + SHIFT], right[KEEP * k : KEEP * k + KEEP]]
        out_ref[i] = jnp.concatenate(rows, axis=0).astype(BF)


def selector():
    token = lax.broadcasted_iota(jnp.int32, (1, LANES), 1)
    column = (token * 1338) >> 16
    cell = token - 49 * column
    slot = 64 * column + cell + 4 * (cell >= 28).astype(jnp.int32) + 4 * (cell >= 40).astype(jnp.int32)
    slot = jnp.where(token < TOKENS, slot, -1)
    place = lax.broadcasted_iota(jnp.int32, (WIN * SLOTS, LANES), 0)
    return (place == slot).astype(F32).astype(BF)


def by_slots(values):
    cells = [values[d] for d in range(WIN)]
    low, high = range(KEEP), range(KEEP, WIN)
    return jnp.concatenate(
        [
            piece_rows(cells, low, (0, KEEP)),
            piece_rows(cells, high, (0, KEEP)),
            piece_rows(cells, low, (KEEP, WIN)),
            piece_rows(cells, high, (KEEP, WIN)),
        ],
        axis=0,
    )


def turned(values):
    return values.astype(F32).T.astype(BF)


def ready_kernel(
    region_ref, labels_ref, g1_ref, g2_ref, qkv_ref, proj_ref, up_ref, downt_ref, head_ref,
    ids_ref, sel_ref, gain1_ref, gain2_ref, qkvt_ref, projt_ref, upt_ref, down_ref, headt_ref, heads_ref,
):
    sel = selector()
    sel_ref[...] = sel
    rows = []
    for ref in (region_ref, labels_ref):
        flat = by_slots(ref[...].astype(F32)).T
        for w in range(WINDOWS):
            rows.append(jnp.concatenate([flat[WIN * w + c : WIN * w + c + 1] for c in range(WIN)], axis=1))
    ids = nn(jnp.concatenate(rows, axis=0).astype(BF), sel)
    token = lax.broadcasted_iota(jnp.int32, ids.shape, 1)
    row = lax.broadcasted_iota(jnp.int32, ids.shape, 0)
    ids_ref[...] = jnp.where(token < TOKENS, ids, jnp.where(row < WINDOWS, 4.0, -1.0))
    for ref, out in ((g1_ref, gain1_ref), (g2_ref, gain2_ref)):
        out[...] = jnp.broadcast_to(ref[...], (128, C)).T
    qkvt_ref[...] = turned(qkv_ref[...])
    projt_ref[...] = turned(proj_ref[...])
    upt_ref[...] = turned(up_ref[...])
    down_ref[...] = turned(downt_ref[...])
    head = jnp.concatenate([head_ref[...].astype(F32), jnp.zeros((2, C), F32)], axis=0)
    headt_ref[...] = head.astype(BF)
    heads_ref[...] = head.T.astype(BF)


def norm(values, gain):
    center = values - jnp.mean(values, axis=0, keepdims=True)
    inverse = lax.rsqrt(jnp.mean(center * center, axis=0, keepdims=True) + 1e-5)
    unit = center * inverse
    return unit, inverse, (unit * gain).astype(BF)


def norm_back(cotangent, unit, inverse, gain):
    scaled = cotangent * gain
    middle = jnp.mean(scaled, axis=0, keepdims=True)
    along = jnp.mean(scaled * unit, axis=0, keepdims=True)
    return inverse * (scaled - middle - unit * along)


def paired(rows, first, second):
    blank = jnp.zeros((HEAD, LANES), BF)
    left = jnp.concatenate([rows[:HEAD], blank, first], axis=0)
    right = jnp.concatenate([blank, rows[HEAD:], second], axis=0)
    return jnp.concatenate([left, right], axis=1)


def blockdiag(rows):
    blank = jnp.zeros((HEAD, LANES), BF)
    first = jnp.concatenate([rows[:HEAD], blank], axis=1)
    second = jnp.concatenate([blank, rows[HEAD:]], axis=1)
    return jnp.concatenate([first, second], axis=0)


def by_columns(rows, weights):
    rows = rows[:, :ROWS]
    left = nn(rows[:HEAD], weights[:, :256])
    middle = nn(rows, weights[:, 256:512])
    right = nn(rows[HEAD:], weights[:, 512:])
    first = jnp.concatenate([left, middle[:HEAD, :128]], axis=1)
    second = jnp.concatenate([middle[HEAD:, 128:], right], axis=1)
    return jnp.concatenate([first, second], axis=0)


def across(ref):
    columns = []
    for w in range(WINDOWS):
        columns.append(jnp.concatenate([ref[PAIRS * w + p] for p in range(PAIRS)], axis=0))
    return jnp.concatenate(columns, axis=1)


def each_pair(values):
    for w in range(WINDOWS):
        for p in range(PAIRS):
            yield PAIRS * w + p, values[32 * p : 32 * p + 32, LANES * w : LANES * w + LANES]


def in_turn(start, finish, buffers):
    first, second = buffers
    last = WINDOWS * PAIRS - 2

    def two(i, carry):
        start(2 * i + 1, *second)
        finish(2 * i, *first)
        start(2 * i + 2, *first)
        finish(2 * i + 1, *second)
        return carry

    start(0, *first)
    lax.fori_loop(0, last // 2, two, 0)
    start(last + 1, *second)
    finish(last, *first)
    finish(last + 1, *second)


def main_kernel(
    scale,
    a_ref, c_ref, d_ref, b_ref, ids_ref, sel_ref, gain1_ref, gain2_ref,
    qkv_ref, qkvt_ref, proj_ref, projt_ref, up_ref, upt_ref, down_ref, downt_ref, head_ref, headt_ref,
    oa_ref, oc_ref, od_ref, ob_ref,
    x_ref, q_ref, k_ref, v_ref, keyst_ref, valuest_ref, side_ref, e_ref, s0_ref, s1_ref, top0_ref, top1_ref,
    attended_ref, inverse_ref, d_hidden_ref, d_mixed_ref, extra_ref, dq_ref, dk_ref, dv_ref, slope_ref,
):
    sel = sel_ref[...]
    pieces = [a_ref[...].astype(F32), unpacked(b_ref, 12), unpacked(c_ref, 12), unpacked(d_ref, 9)]
    rows = jnp.concatenate(pieces, axis=0)
    tall = rows.T
    for w in range(WINDOWS):
        cols = [(WIN * w + SHIFT + c) % NX for c in range(WIN)]
        wide = jnp.concatenate([tall[C * c : C * c + C] for c in cols], axis=1).astype(BF)
        x_ref[:, LANES * w : LANES * w + LANES] = nn(wide, sel)
    dk_ref[...] = jnp.zeros(dk_ref.shape, BF)
    dv_ref[...] = jnp.zeros(dv_ref.shape, BF)

    gain1 = jnp.concatenate([gain1_ref[...]] * (3 * WINDOWS), axis=1)
    gain2 = jnp.concatenate([gain2_ref[...]] * (3 * WINDOWS), axis=1)
    unit1, inverse1, normed1 = norm(x_ref[...], gain1)
    index = lax.broadcasted_iota(jnp.int32, (16, LANES), 0)
    ones = jnp.where(index < 2, 1.0, 0.0).astype(BF)
    key_sides = []
    for w in range(WINDOWS):
        same = index.astype(F32) == ids_ref[w : w + 1, :]
        key_sides.append(same.astype(F32).astype(BF))
        side_ref[w] = jnp.where(same | (index > 4), 0.0, FAR).astype(BF)
    for t, part in each_pair((nn(qkvt_ref[:C, :], normed1) * (0.25 * LOG2E)).astype(BF)):
        q_ref[t] = part
    for t, part in each_pair(nn(qkvt_ref[C : 2 * C, :], normed1).astype(BF)):
        k_ref[t] = part
        keyst_ref[t] = turned(jnp.concatenate([part, key_sides[t // PAIRS]], axis=0))[:ROWS]
    for t, part in each_pair(nn(qkvt_ref[2 * C :, :], normed1).astype(BF)):
        v_ref[t] = part
        valuest_ref[t] = turned(jnp.concatenate([part, ones], axis=0))[:ROWS]

    def score(t, out_ref, top_ref):
        side = side_ref[lax.div(t, PAIRS)]
        scores = nn(keyst_ref[t], paired(q_ref[t], side, side))
        out_ref[...] = scores
        top_ref[0:1, :] = jnp.max(scores, axis=0, keepdims=True)

    def mix(t, in_ref, top_ref):
        powers = jnp.exp2(in_ref[...] - top_ref[0:1, :])
        raised = powers.astype(BF)
        e_ref[t] = raised
        inverse_sum = 1.0 / jnp.sum(powers, axis=0, keepdims=True)
        sums = []
        for h in range(2):
            part = inverse_sum[:, LANES * h : LANES * h + LANES]
            inverse_ref[t, h : h + 1, :] = part
            sums.append(jnp.broadcast_to(part, (HEAD, LANES)))
        attended_ref[t] = (by_columns(v_ref[t], raised) * jnp.concatenate(sums, axis=0)).astype(BF)

    buffers = ((s0_ref, top0_ref), (s1_ref, top1_ref))
    in_turn(score, mix, buffers)

    attended = across(attended_ref)
    hidden = x_ref[...] + nn(projt_ref[...], attended)
    unit2, inverse2, normed2 = norm(hidden, gain2)
    output = hidden
    for j in range(3):
        part = slice(128 * j, 128 * j + 128)
        raised = nn(upt_ref[part, :], normed2)
        below = 0.5 + 0.5 * lax.erf(raised * (0.5**0.5))
        bell = jnp.exp(-0.5 * raised * raised) * 0.3989422804014327
        slope_ref[part, :] = below + raised * bell
        output = output + nn(downt_ref[:, part], (raised * below).astype(BF))
    logits = nn(headt_ref[...], output.astype(BF))
    labels = jnp.concatenate([ids_ref[WINDOWS + w : WINDOWS + w + 1, :] for w in range(WINDOWS)], axis=1)
    kind = lax.broadcasted_iota(jnp.int32, (16, WINDOWS * LANES), 0)
    logits = jnp.where(kind < CLASSES, logits, -1e30)
    powers = jnp.exp(logits - jnp.max(logits, axis=0, keepdims=True))
    soft = powers / jnp.sum(powers, axis=0, keepdims=True)
    at_label = (kind.astype(F32) == labels).astype(F32)
    d_logits = jnp.where(labels >= 0.0, (soft - at_label) * scale, 0.0)
    d_output = nn(head_ref[...], d_logits.astype(BF)).astype(BF)
    d_normed2 = jnp.zeros((C, WINDOWS * LANES), F32)
    for j in range(3):
        part = slice(128 * j, 128 * j + 128)
        d_expanded = nn(down_ref[part, :], d_output)
        d_raised = (d_expanded * slope_ref[part, :]).astype(BF)
        d_normed2 = d_normed2 + nn(up_ref[:, part], d_raised)
    d_hidden = d_output.astype(F32) + norm_back(d_normed2, unit2, inverse2, gain2)
    d_hidden_ref[...] = d_hidden
    d_attended = nn(proj_ref[...], d_hidden.astype(BF))
    for h in range(HEADS):
        own = slice(HEAD * h, HEAD * h + HEAD)
        sums = jnp.concatenate(
            [inverse_ref[PAIRS * w + h // 2, h % 2 : h % 2 + 1, :] for w in range(WINDOWS)], axis=1
        )
        d_mixed = (d_attended[own] * sums).astype(BF)
        along = -jnp.sum(d_mixed.astype(F32) * attended[own].astype(F32), axis=0, keepdims=True)
        coarse = along.astype(BF).astype(F32)
        rest = along - coarse
        place = slice(HEAD * (h % 2), HEAD * (h % 2) + HEAD)
        for w in range(WINDOWS):
            lanes = slice(LANES * w, LANES * w + LANES)
            d_mixed_ref[PAIRS * w + h // 2, place, :] = d_mixed[:, lanes]
            extra = jnp.where(index == 0, coarse[:, lanes], jnp.where(index == 1, rest[:, lanes], 0.0))
            extra_ref[PAIRS * w + h // 2, place, :] = extra.astype(BF)

    def weigh(t, out_ref, unused):
        extra = extra_ref[t]
        out_ref[...] = nn(valuest_ref[t], paired(d_mixed_ref[t], extra[:HEAD], extra[HEAD:]))

    def unmix(t, in_ref, unused):
        raised = e_ref[t]
        d_scores = (raised.astype(F32) * in_ref[...]).astype(BF)
        dv_ref[t, :, :ROWS] = nt(raised, blockdiag(d_mixed_ref[t])).T.astype(BF)
        dq_ref[t] = (by_columns(k_ref[t], d_scores) * 0.25).astype(BF)
        dk_ref[t, :, :ROWS] = (nt(d_scores, blockdiag(q_ref[t])).T * LN2).astype(BF)

    in_turn(weigh, unmix, buffers)

    d_normed1 = nn(qkv_ref[...], jnp.concatenate([across(r) for r in (dq_ref, dk_ref, dv_ref)], axis=0))
    unit1, inverse1, normed1 = norm(x_ref[...], gain1)
    grad = (d_hidden_ref[...] + norm_back(d_normed1, unit1, inverse1, gain1)).astype(BF)
    blocks = [None] * NX
    for w in range(WINDOWS):
        wide = nt(grad[:, LANES * w : LANES * w + LANES], sel)
        for c in range(WIN):
            blocks[(WIN * w + SHIFT + c) % NX] = wide[:, SLOTS * c : SLOTS * c + SLOTS]
    rows = jnp.concatenate(blocks, axis=0).T
    oa_ref[...] = rows[:16].astype(BF)
    for k, (ref, count) in enumerate(((ob_ref, 12), (oc_ref, 12), (od_ref, 9))):
        ref[...] = packed(rows[16 * k + 16 : 16 * k + 32], count)


VMEM = pl.BlockSpec(memory_space=pltpu.VMEM)
SMALL = pltpu.CompilerParams(vmem_limit_bytes=8 * 2**20)
PIECES = [jax.ShapeDtypeStruct(s, BF) for s in ((16, WIDE), (8, 4096), (8, 3072), (8, 4096))]


def cut(features):
    return pl.pallas_call(cut_kernel, out_shape=PIECES, in_specs=[VMEM], out_specs=[VMEM] * 4, compiler_params=SMALL)(features)


def join(*pieces):
    out = jax.ShapeDtypeStruct((WIN, WIN, WIDE), BF)
    return pl.pallas_call(join_kernel, out_shape=out, in_specs=[VMEM] * 4, out_specs=VMEM, compiler_params=SMALL)(*pieces)


def ready(region, labels, attn_gain, mlp_gain, qkv_weight, proj_weight, up_weight, down_weight, head_weight):
    S = jax.ShapeDtypeStruct
    out = [
        S((8, LANES), F32), S((WIN * SLOTS, LANES), BF), S((C, 128), F32), S((C, 128), F32),
        S((3 * C, C), BF), S((C, C), BF), S((HID, C), BF), S((HID, C), BF), S((16, C), BF), S((C, 16), BF),
    ]
    return pl.pallas_call(ready_kernel, out_shape=out, in_specs=[VMEM] * 9, out_specs=[VMEM] * 10, compiler_params=SMALL)(
        region, labels, attn_gain.reshape(1, C), mlp_gain.reshape(1, C),
        qkv_weight, proj_weight, up_weight, down_weight, head_weight,
    )


def gradient(pieces, prepared, weights, scale):
    ids, sel, gain1, gain2, qkv_t, proj_t, up_t, down, head_t, head = prepared
    qkv_weight, proj_weight, up_weight, down_t = weights
    return pl.pallas_call(
        functools.partial(main_kernel, scale),
        out_shape=PIECES,
        in_specs=[VMEM] * 18,
        out_specs=[VMEM] * 4,
        scratch_shapes=[
            pltpu.VMEM((C, WINDOWS * LANES), F32),
            pltpu.VMEM((12, 32, LANES), BF),
            pltpu.VMEM((12, 32, LANES), BF),
            pltpu.VMEM((12, 32, LANES), BF),
            pltpu.VMEM((12, ROWS, 48), BF),
            pltpu.VMEM((12, ROWS, 48), BF),
            pltpu.VMEM((WINDOWS, 16, LANES), BF),
            pltpu.VMEM((12, ROWS, 2 * LANES), BF),
            pltpu.VMEM((ROWS, 2 * LANES), F32),
            pltpu.VMEM((ROWS, 2 * LANES), F32),
            pltpu.VMEM((8, 2 * LANES), F32),
            pltpu.VMEM((8, 2 * LANES), F32),
            pltpu.VMEM((12, 32, LANES), BF),
            pltpu.VMEM((12, 8, LANES), F32),
            pltpu.VMEM((C, WINDOWS * LANES), F32),
            pltpu.VMEM((12, 32, LANES), BF),
            pltpu.VMEM((12, 32, LANES), BF),
            pltpu.VMEM((12, 32, LANES), BF),
            pltpu.VMEM((12, 32, LANES), BF),
            pltpu.VMEM((12, 32, LANES), BF),
            pltpu.VMEM((HID, WINDOWS * LANES), F32),
        ],
        compiler_params=pltpu.CompilerParams(vmem_limit_bytes=32 * 2**20),
    )(
        *pieces, ids, sel, gain1, gain2, qkv_weight, qkv_t, proj_weight, proj_t,
        up_weight, up_t, down, down_t, head, head_t,
    )


def moved(piece, axes, steps):
    sizes = [lax.axis_size(a) for a in axes]
    route = []
    if len(axes) == 1:
        (n,) = sizes
        route = [((i - steps) % n, i) for i in range(n)]
    else:
        n, m = sizes
        for i in range(n):
            for j in range(m):
                route.append((((i - steps) % n) * m + (j - steps) % m, i * m + j))
    return lax.ppermute(piece, axes if len(axes) > 1 else axes[0], route)


ROADS = (("gy",), ("gz", "gy"), ("gz",))


def body(
    features, region, labels, attn_gain, qkv_weight, proj_weight, mlp_gain, up_weight, down_weight, head_weight,
):
    own, *away = cut(features)
    down_t = down_weight.T
    arrived = [moved(piece, road, -1) for piece, road in zip(away, ROADS)]
    prepared = ready(
        region, labels, attn_gain, mlp_gain, qkv_weight, proj_weight, up_weight, down_t, head_weight.T
    )
    scale = 1.0 / (WIN * WIN * NX * lax.axis_size("gz") * lax.axis_size("gy"))
    own, *away = gradient((own, *arrived), prepared, (qkv_weight, proj_weight, up_weight, down_t), scale)
    arrived = [moved(piece, road, 1) for piece, road in zip(away, ROADS)]
    return join(own, *arrived)


def solution(mesh):
    cells = P("gz", "gy", None)
    in_specs = (cells, cells, cells) + (P(),) * 7
    return jax.shard_map(body, mesh=mesh, in_specs=in_specs, out_specs=cells, check_vma=False)
```

```python
import functools

import jax
import jax.numpy as jnp
from jax import lax
from jax.experimental import pallas as pl
from jax.experimental.pallas import tpu as pltpu
from jax.sharding import PartitionSpec as P

C = 96
HEADS = 6
HEAD = 16
HID = 384
CLASSES = 14
WIN = 7
SHIFT = 3
KEEP = WIN - SHIFT
NX = 28
WINDOWS = 4
TOKENS = 343
LANES = 384
ROWS = 352
PAIRS = 3
SLOTS = 64
WIDE = NX * C
HALF = 1408
FAR = -(2.0**30)
LOG2E = 1.4426950408889634
LN2 = 0.6931471805599453
BF = jnp.bfloat16
F32 = jnp.float32


def nn(a, b):
    return lax.dot_general(a, b, (((1,), (0,)), ((), ())), preferred_element_type=F32)


def nt(a, b):
    return lax.dot_general(a, b, (((1,), (1,)), ((), ())), preferred_element_type=F32)


def piece_rows(cells, depths, rows):
    parts = [cells[d][rows[0] : rows[1]] for d in depths]
    used = len(depths) * (rows[1] - rows[0])
    if used < 16:
        parts.append(jnp.zeros((16 - used, parts[0].shape[1]), parts[0].dtype))
    return jnp.concatenate(parts, axis=0)


def packed(rows, count):
    if count == 12:
        rest = rows[8:12]
        last = jnp.concatenate([rest[:, HALF:], jnp.zeros((4, 2 * HALF - WIDE), F32)], axis=1)
        tail = jnp.concatenate([rest[:, :HALF], last], axis=0)
    else:
        parts = [rows[8:9, LANES * k : LANES * k + LANES] for k in range(WIN)]
        tail = jnp.concatenate(parts + [jnp.zeros((1, LANES), F32)], axis=0)
    return jnp.concatenate([rows[:8], tail], axis=1).astype(BF)


def halved(values, first, second):
    first[...] = values[:, :2048]
    second[...] = values[:, 2048:]


def whole_of(first, second):
    return jnp.concatenate([first[...], second[...]], axis=1)


def unpacked(ref, count):
    values = ref[...].astype(F32)
    tail = values[:, WIDE:]
    if count == 12:
        rest = jnp.concatenate([tail[:4], tail[4:8, : WIDE - HALF]], axis=1)
    else:
        rest = jnp.concatenate([tail[k : k + 1] for k in range(WIN)], axis=1)
    blank = jnp.zeros((16 - count, WIDE), F32)
    return jnp.concatenate([values[:, :WIDE], rest, blank], axis=0)


def cut_kernel(f_ref, a_ref, c_ref, d_ref, b_ref, b2_ref):
    cells = [f_ref[d].astype(F32) for d in range(WIN)]
    low, high = range(SHIFT), range(SHIFT, WIN)
    a_ref[...] = piece_rows(cells, high, (SHIFT, WIN)).astype(BF)
    halved(packed(piece_rows(cells, low, (SHIFT, WIN)), 12), b_ref, b2_ref)
    c_ref[...] = packed(piece_rows(cells, high, (0, SHIFT)), 12)
    d_ref[...] = packed(piece_rows(cells, low, (0, SHIFT)), 9)


def join_kernel(a_ref, c_ref, d_ref, b_ref, b2_ref, out_ref):
    a = a_ref[...].astype(F32)
    b = unpacked(whole_of(b_ref, b2_ref), 12)
    c = unpacked(c_ref, 12)
    d = unpacked(d_ref, 9)
    for i in range(WIN):
        if i < SHIFT:
            left, right, k = d, b, i
        else:
            left, right, k = c, a, i - SHIFT
        rows = [left[SHIFT * k : SHIFT * k + SHIFT], right[KEEP * k : KEEP * k + KEEP]]
        out_ref[i] = jnp.concatenate(rows, axis=0).astype(BF)


def selector():
    token = lax.broadcasted_iota(jnp.int32, (1, LANES), 1)
    column = (token * 1338) >> 16
    cell = token - 49 * column
    slot = 64 * column + cell + 4 * (cell >= 28).astype(jnp.int32) + 4 * (cell >= 40).astype(jnp.int32)
    slot = jnp.where(token < TOKENS, slot, -1)
    place = lax.broadcasted_iota(jnp.int32, (WIN * SLOTS, LANES), 0)
    return (place == slot).astype(F32).astype(BF)


def by_slots(values):
    cells = [values[d] for d in range(WIN)]
    low, high = range(KEEP), range(KEEP, WIN)
    return jnp.concatenate(
        [
            piece_rows(cells, low, (0, KEEP)),
            piece_rows(cells, high, (0, KEEP)),
            piece_rows(cells, low, (KEEP, WIN)),
            piece_rows(cells, high, (KEEP, WIN)),
        ],
        axis=0,
    )


def turned(values):
    return values.astype(F32).T.astype(BF)


def ready_kernel(
    region_ref, labels_ref, g1_ref, g2_ref, qkv_ref, proj_ref, up_ref, downt_ref, head_ref,
    ids_ref, sel_ref, gain1_ref, gain2_ref, qkvt_ref, projt_ref, upt_ref, down_ref, headt_ref, heads_ref,
):
    sel = selector()
    sel_ref[...] = sel
    rows = []
    for ref in (region_ref, labels_ref):
        flat = by_slots(ref[...].astype(F32)).T
        for w in range(WINDOWS):
            rows.append(jnp.concatenate([flat[WIN * w + c : WIN * w + c + 1] for c in range(WIN)], axis=1))
    ids = nn(jnp.concatenate(rows, axis=0).astype(BF), sel)
    token = lax.broadcasted_iota(jnp.int32, ids.shape, 1)
    row = lax.broadcasted_iota(jnp.int32, ids.shape, 0)
    ids_ref[...] = jnp.where(token < TOKENS, ids, jnp.where(row < WINDOWS, 4.0, -1.0))
    for ref, out in ((g1_ref, gain1_ref), (g2_ref, gain2_ref)):
        out[...] = jnp.broadcast_to(ref[...], (128, C)).T
    qkvt_ref[...] = turned(qkv_ref[...])
    projt_ref[...] = turned(proj_ref[...])
    upt_ref[...] = turned(up_ref[...])
    down_ref[...] = turned(downt_ref[...])
    head = jnp.concatenate([head_ref[...].astype(F32), jnp.zeros((2, C), F32)], axis=0)
    headt_ref[...] = head.astype(BF)
    heads_ref[...] = head.T.astype(BF)


def norm(values, gain):
    center = values - jnp.mean(values, axis=0, keepdims=True)
    inverse = lax.rsqrt(jnp.mean(center * center, axis=0, keepdims=True) + 1e-5)
    unit = center * inverse
    return unit, inverse, (unit * gain).astype(BF)


def norm_back(cotangent, unit, inverse, gain):
    scaled = cotangent * gain
    middle = jnp.mean(scaled, axis=0, keepdims=True)
    along = jnp.mean(scaled * unit, axis=0, keepdims=True)
    return inverse * (scaled - middle - unit * along)


def paired(rows, first, second):
    blank = jnp.zeros((HEAD, LANES), BF)
    left = jnp.concatenate([rows[:HEAD], blank, first], axis=0)
    right = jnp.concatenate([blank, rows[HEAD:], second], axis=0)
    return jnp.concatenate([left, right], axis=1)


def blockdiag(rows):
    blank = jnp.zeros((HEAD, LANES), BF)
    first = jnp.concatenate([rows[:HEAD], blank], axis=1)
    second = jnp.concatenate([blank, rows[HEAD:]], axis=1)
    return jnp.concatenate([first, second], axis=0)


def by_columns(rows, weights):
    rows = rows[:, :ROWS]
    left = nn(rows[:HEAD], weights[:, :256])
    middle = nn(rows, weights[:, 256:512])
    right = nn(rows[HEAD:], weights[:, 512:])
    first = jnp.concatenate([left, middle[:HEAD, :128]], axis=1)
    second = jnp.concatenate([middle[HEAD:, 128:], right], axis=1)
    return jnp.concatenate([first, second], axis=0)


def across(ref):
    columns = []
    for w in range(WINDOWS):
        columns.append(jnp.concatenate([ref[PAIRS * w + p] for p in range(PAIRS)], axis=0))
    return jnp.concatenate(columns, axis=1)


def each_pair(values):
    for w in range(WINDOWS):
        for p in range(PAIRS):
            yield PAIRS * w + p, values[32 * p : 32 * p + 32, LANES * w : LANES * w + LANES]


def in_turn(start, finish, buffers):
    first, second = buffers
    last = WINDOWS * PAIRS - 2

    def two(i, carry):
        start(2 * i + 1, *second)
        finish(2 * i, *first)
        start(2 * i + 2, *first)
        finish(2 * i + 1, *second)
        return carry

    start(0, *first)
    lax.fori_loop(0, last // 2, two, 0, unroll=5)
    start(last + 1, *second)
    finish(last, *first)
    finish(last + 1, *second)


def main_kernel(
    scale,
    a_ref, c_ref, d_ref, b_ref, b2_ref, ids_ref, sel_ref, gain1_ref, gain2_ref,
    qkv_ref, qkvt_ref, proj_ref, projt_ref, up_ref, upt_ref, down_ref, downt_ref, head_ref, headt_ref,
    oa_ref, oc_ref, od_ref, ob_ref, ob2_ref,
    x_ref, unit1_ref, inverse1_ref, q_ref, k_ref, v_ref, keyst_ref, valuest_ref, side_ref, e_ref, s0_ref, s1_ref, top0_ref, top1_ref,
    attended_ref, inverse_ref, d_hidden_ref, d_mixed_ref, extra_ref, dq_ref, dk_ref, dv_ref, slope_ref,
):
    sel = sel_ref[...]
    pieces = [a_ref[...].astype(F32), unpacked(whole_of(b_ref, b2_ref), 12), unpacked(c_ref, 12), unpacked(d_ref, 9)]
    rows = jnp.concatenate(pieces, axis=0)
    tall = rows.T
    wides = []
    for w in range(WINDOWS):
        cols = [(WIN * w + SHIFT + c) % NX for c in range(WIN)]
        wides.append(jnp.concatenate([tall[C * c : C * c + C] for c in cols], axis=1).astype(BF))
    stacked = nn(jnp.concatenate(wides, axis=0), sel)
    x = jnp.concatenate([stacked[C * w : C * w + C] for w in range(WINDOWS)], axis=1)
    x_ref[...] = x
    dk_ref[...] = jnp.zeros(dk_ref.shape, BF)
    dv_ref[...] = jnp.zeros(dv_ref.shape, BF)

    gain1 = jnp.concatenate([gain1_ref[...]] * (3 * WINDOWS), axis=1)
    gain2 = jnp.concatenate([gain2_ref[...]] * (3 * WINDOWS), axis=1)
    unit1, inverse1, normed1 = norm(x, gain1)
    unit1_ref[...] = unit1
    inverse1_ref[0:1, :] = inverse1
    index = lax.broadcasted_iota(jnp.int32, (16, LANES), 0)
    ones = jnp.where(index < 2, 1.0, 0.0).astype(BF)
    key_sides = []
    for w in range(WINDOWS):
        same = index.astype(F32) == ids_ref[w : w + 1, :]
        key_sides.append(same.astype(F32).astype(BF))
        side_ref[w] = jnp.where(same | (index > 4), 0.0, FAR).astype(BF)
    for t, part in each_pair((nn(qkvt_ref[:C, :], normed1) * (0.25 * LOG2E)).astype(BF)):
        q_ref[t] = part
    for t, part in each_pair(nn(qkvt_ref[C : 2 * C, :], normed1).astype(BF)):
        k_ref[t] = part
        keyst_ref[t] = turned(jnp.concatenate([part, key_sides[t // PAIRS]], axis=0))[:ROWS]
    for t, part in each_pair(nn(qkvt_ref[2 * C :, :], normed1).astype(BF)):
        v_ref[t] = part
        valuest_ref[t] = turned(jnp.concatenate([part, ones], axis=0))[:ROWS]

    def score(t, out_ref, top_ref):
        side = side_ref[lax.div(t, PAIRS)]
        scores = nn(keyst_ref[t], paired(q_ref[t], side, side))
        out_ref[...] = scores
        top_ref[0:1, :] = jnp.max(scores, axis=0, keepdims=True)

    def mix(t, in_ref, top_ref):
        powers = jnp.exp2(in_ref[...] - top_ref[0:1, :])
        raised = powers.astype(BF)
        e_ref[t] = raised
        inverse_sum = 1.0 / jnp.sum(powers, axis=0, keepdims=True)
        sums = []
        for h in range(2):
            part = inverse_sum[:, LANES * h : LANES * h + LANES]
            inverse_ref[t, h : h + 1, :] = part
            sums.append(jnp.broadcast_to(part, (HEAD, LANES)))
        attended_ref[t] = (by_columns(v_ref[t], raised) * jnp.concatenate(sums, axis=0)).astype(BF)

    buffers = ((s0_ref, top0_ref), (s1_ref, top1_ref))
    in_turn(score, mix, buffers)

    attended = across(attended_ref)
    hidden = x_ref[...] + nn(projt_ref[...], attended)
    unit2, inverse2, normed2 = norm(hidden, gain2)
    output = hidden
    for j in range(3):
        part = slice(128 * j, 128 * j + 128)
        raised = nn(upt_ref[part, :], normed2)
        inner = raised * (0.5**0.5)
        below = 0.5 + 0.5 * lax.erf(inner)
        bell = jnp.exp2(inner * inner * -LOG2E)
        slope_ref[part, :] = below + (raised * 0.3989422804014327) * bell
        output = output + nn(downt_ref[:, part], (raised * below).astype(BF))
    logits = nn(headt_ref[...], output.astype(BF))
    labels = jnp.concatenate([ids_ref[WINDOWS + w : WINDOWS + w + 1, :] for w in range(WINDOWS)], axis=1)
    kind = lax.broadcasted_iota(jnp.int32, (16, WINDOWS * LANES), 0)
    logits = jnp.where(kind < CLASSES, logits, -1e30)
    powers = jnp.exp(logits - jnp.max(logits, axis=0, keepdims=True))
    soft = powers / jnp.sum(powers, axis=0, keepdims=True)
    at_label = (kind.astype(F32) == labels).astype(F32)
    d_logits = jnp.where(labels >= 0.0, (soft - at_label) * scale, 0.0)
    d_output = nn(head_ref[...], d_logits.astype(BF)).astype(BF)
    d_normed2 = jnp.zeros((C, WINDOWS * LANES), F32)
    for j in range(3):
        part = slice(128 * j, 128 * j + 128)
        d_expanded = nn(down_ref[part, :], d_output)
        d_raised = (d_expanded * slope_ref[part, :]).astype(BF)
        d_normed2 = d_normed2 + nn(up_ref[:, part], d_raised)
    d_hidden = d_output.astype(F32) + norm_back(d_normed2, unit2, inverse2, gain2)
    d_hidden_ref[...] = d_hidden
    d_attended = nn(proj_ref[...], d_hidden.astype(BF))
    for h in range(HEADS):
        own = slice(HEAD * h, HEAD * h + HEAD)
        sums = jnp.concatenate(
            [inverse_ref[PAIRS * w + h // 2, h % 2 : h % 2 + 1, :] for w in range(WINDOWS)], axis=1
        )
        d_mixed = (d_attended[own] * sums).astype(BF)
        along = -jnp.sum(d_mixed.astype(F32) * attended[own].astype(F32), axis=0, keepdims=True)
        coarse = along.astype(BF).astype(F32)
        rest = along - coarse
        place = slice(HEAD * (h % 2), HEAD * (h % 2) + HEAD)
        for w in range(WINDOWS):
            lanes = slice(LANES * w, LANES * w + LANES)
            d_mixed_ref[PAIRS * w + h // 2, place, :] = d_mixed[:, lanes]
            extra = jnp.where(index == 0, coarse[:, lanes], jnp.where(index == 1, rest[:, lanes], 0.0))
            extra_ref[PAIRS * w + h // 2, place, :] = extra.astype(BF)

    def weigh(t, out_ref, unused):
        extra = extra_ref[t]
        out_ref[...] = nn(valuest_ref[t], paired(d_mixed_ref[t], extra[:HEAD], extra[HEAD:]))

    def unmix(t, in_ref, unused):
        raised = e_ref[t]
        d_scores = (raised.astype(F32) * in_ref[...]).astype(BF)
        dv_ref[t, :, :ROWS] = nt(blockdiag(d_mixed_ref[t]), raised).astype(BF)
        dq_ref[t] = (by_columns(k_ref[t], d_scores) * 0.25).astype(BF)
        dk_ref[t, :, :ROWS] = (nt(d_scores, blockdiag(q_ref[t])).T * LN2).astype(BF)

    in_turn(weigh, unmix, buffers)

    d_normed1 = nn(qkv_ref[...], jnp.concatenate([across(r) for r in (dq_ref, dk_ref, dv_ref)], axis=0))
    unit1, inverse1 = unit1_ref[...], inverse1_ref[0:1, :]
    grad = (d_hidden_ref[...] + norm_back(d_normed1, unit1, inverse1, gain1)).astype(BF)
    blocks = [None] * NX
    stacked = nt(jnp.concatenate([grad[:, LANES * w : LANES * w + LANES] for w in range(WINDOWS)], axis=0), sel)
    for w in range(WINDOWS):
        wide = stacked[C * w : C * w + C]
        for c in range(WIN):
            blocks[(WIN * w + SHIFT + c) % NX] = wide[:, SLOTS * c : SLOTS * c + SLOTS]
    rows = jnp.concatenate(blocks, axis=0).T
    oa_ref[...] = rows[:16].astype(BF)
    halved(packed(rows[16:32], 12), ob_ref, ob2_ref)
    oc_ref[...] = packed(rows[32:48], 12)
    od_ref[...] = packed(rows[48:], 9)


VMEM = pl.BlockSpec(memory_space=pltpu.VMEM)
SMALL = pltpu.CompilerParams(vmem_limit_bytes=8 * 2**20)
PIECES = [jax.ShapeDtypeStruct(s, BF) for s in ((16, WIDE), (8, 4096), (8, 3072), (8, 2048), (8, 2048))]


def cut(features):
    return pl.pallas_call(cut_kernel, out_shape=PIECES, in_specs=[VMEM], out_specs=[VMEM] * 5, compiler_params=SMALL)(features)


def join(*pieces):
    out = jax.ShapeDtypeStruct((WIN, WIN, WIDE), BF)
    return pl.pallas_call(join_kernel, out_shape=out, in_specs=[VMEM] * 5, out_specs=VMEM, compiler_params=SMALL)(*pieces)


def ready(region, labels, attn_gain, mlp_gain, qkv_weight, proj_weight, up_weight, down_weight, head_weight):
    S = jax.ShapeDtypeStruct
    out = [
        S((8, LANES), F32), S((WIN * SLOTS, LANES), BF), S((C, 128), F32), S((C, 128), F32),
        S((3 * C, C), BF), S((C, C), BF), S((HID, C), BF), S((HID, C), BF), S((16, C), BF), S((C, 16), BF),
    ]
    return pl.pallas_call(ready_kernel, out_shape=out, in_specs=[VMEM] * 9, out_specs=[VMEM] * 10, compiler_params=SMALL)(
        region, labels, attn_gain.reshape(1, C), mlp_gain.reshape(1, C),
        qkv_weight, proj_weight, up_weight, down_weight, head_weight,
    )


def gradient(pieces, prepared, weights, scale):
    ids, sel, gain1, gain2, qkv_t, proj_t, up_t, down, head_t, head = prepared
    qkv_weight, proj_weight, up_weight, down_t = weights
    return pl.pallas_call(
        functools.partial(main_kernel, scale),
        out_shape=PIECES,
        in_specs=[VMEM] * 19,
        out_specs=[VMEM] * 5,
        scratch_shapes=[
            pltpu.VMEM((C, WINDOWS * LANES), F32),
            pltpu.VMEM((C, WINDOWS * LANES), F32),
            pltpu.VMEM((8, WINDOWS * LANES), F32),
            pltpu.VMEM((12, 32, LANES), BF),
            pltpu.VMEM((12, 32, LANES), BF),
            pltpu.VMEM((12, 32, LANES), BF),
            pltpu.VMEM((12, ROWS, 48), BF),
            pltpu.VMEM((12, ROWS, 48), BF),
            pltpu.VMEM((WINDOWS, 16, LANES), BF),
            pltpu.VMEM((12, ROWS, 2 * LANES), BF),
            pltpu.VMEM((ROWS, 2 * LANES), F32),
            pltpu.VMEM((ROWS, 2 * LANES), F32),
            pltpu.VMEM((8, 2 * LANES), F32),
            pltpu.VMEM((8, 2 * LANES), F32),
            pltpu.VMEM((12, 32, LANES), BF),
            pltpu.VMEM((12, 8, LANES), F32),
            pltpu.VMEM((C, WINDOWS * LANES), F32),
            pltpu.VMEM((12, 32, LANES), BF),
            pltpu.VMEM((12, 32, LANES), BF),
            pltpu.VMEM((12, 32, LANES), BF),
            pltpu.VMEM((12, 32, LANES), BF),
            pltpu.VMEM((12, 32, LANES), BF),
            pltpu.VMEM((HID, WINDOWS * LANES), F32),
        ],
        compiler_params=pltpu.CompilerParams(vmem_limit_bytes=32 * 2**20),
    )(
        *pieces, ids, sel, gain1, gain2, qkv_weight, qkv_t, proj_weight, proj_t,
        up_weight, up_t, down, down_t, head, head_t,
    )


def moved(piece, axes, steps):
    sizes = [lax.axis_size(a) for a in axes]
    route = []
    if len(axes) == 1:
        (n,) = sizes
        route = [((i - steps) % n, i) for i in range(n)]
    else:
        n, m = sizes
        for i in range(n):
            for j in range(m):
                route.append((((i - steps) % n) * m + (j - steps) % m, i * m + j))
    return lax.ppermute(piece, axes if len(axes) > 1 else axes[0], route)


ROADS = (("gy",), ("gz", "gy"), ("gz",), ("gz",))


def body(
    features, region, labels, attn_gain, qkv_weight, proj_weight, mlp_gain, up_weight, down_weight, head_weight,
):
    own, *away = cut(features)
    down_t = down_weight.T
    arrived = [moved(piece, road, -1) for piece, road in zip(away, ROADS)]
    prepared = ready(
        region, labels, attn_gain, mlp_gain, qkv_weight, proj_weight, up_weight, down_t, head_weight.T
    )
    scale = 1.0 / (WIN * WIN * NX * lax.axis_size("gz") * lax.axis_size("gy"))
    own, *away = gradient((own, *arrived), prepared, (qkv_weight, proj_weight, up_weight, down_t), scale)
    arrived = [moved(piece, road, 1) for piece, road in zip(away, ROADS)]
    return join(own, *arrived)


def solution(mesh):
    cells = P("gz", "gy", None)
    in_specs = (cells, cells, cells) + (P(),) * 7
    return jax.shard_map(body, mesh=mesh, in_specs=in_specs, out_specs=cells, check_vma=False)
```

```python
import functools

import jax
import jax.numpy as jnp
from jax import lax
from jax.experimental import pallas as pl
from jax.experimental.pallas import tpu as pltpu
from jax.sharding import PartitionSpec as P

C = 96
HEADS = 6
HEAD = 16
HID = 384
CLASSES = 14
WIN = 7
SHIFT = 3
KEEP = WIN - SHIFT
NX = 28
WINDOWS = 4
TOKENS = 343
LANES = 384
ROWS = 352
PAIRS = 3
SLOTS = 64
WIDE = NX * C
HALF = 1408
FAR = -(2.0**30)
LOG2E = 1.4426950408889634
LN2 = 0.6931471805599453
BF = jnp.bfloat16
F32 = jnp.float32


def nn(a, b):
    return lax.dot_general(a, b, (((1,), (0,)), ((), ())), preferred_element_type=F32)


def nt(a, b):
    return lax.dot_general(a, b, (((1,), (1,)), ((), ())), preferred_element_type=F32)


def piece_rows(cells, depths, rows):
    parts = [cells[d][rows[0] : rows[1]] for d in depths]
    used = len(depths) * (rows[1] - rows[0])
    if used < 16:
        parts.append(jnp.zeros((16 - used, parts[0].shape[1]), parts[0].dtype))
    return jnp.concatenate(parts, axis=0)


def packed(rows, count):
    if count == 12:
        rest = rows[8:12]
        last = jnp.concatenate([rest[:, HALF:], jnp.zeros((4, 2 * HALF - WIDE), F32)], axis=1)
        tail = jnp.concatenate([rest[:, :HALF], last], axis=0)
    else:
        parts = [rows[8:9, LANES * k : LANES * k + LANES] for k in range(WIN)]
        tail = jnp.concatenate(parts + [jnp.zeros((1, LANES), F32)], axis=0)
    return jnp.concatenate([rows[:8], tail], axis=1).astype(BF)


def halved(values, first, second):
    first[...] = values[:, :2048]
    second[...] = values[:, 2048:]


def whole_of(first, second):
    return jnp.concatenate([first[...], second[...]], axis=1)


def unpacked(ref, count):
    values = ref[...].astype(F32)
    tail = values[:, WIDE:]
    if count == 12:
        rest = jnp.concatenate([tail[:4], tail[4:8, : WIDE - HALF]], axis=1)
    else:
        rest = jnp.concatenate([tail[k : k + 1] for k in range(WIN)], axis=1)
    blank = jnp.zeros((16 - count, WIDE), F32)
    return jnp.concatenate([values[:, :WIDE], rest, blank], axis=0)


def cut_kernel(f_ref, a_ref, d_ref, c_ref, c2_ref, b_ref, b2_ref):
    cells = [f_ref[d].astype(F32) for d in range(WIN)]
    low, high = range(SHIFT), range(SHIFT, WIN)
    a_ref[...] = piece_rows(cells, high, (SHIFT, WIN)).astype(BF)
    halved(packed(piece_rows(cells, low, (SHIFT, WIN)), 12), b_ref, b2_ref)
    halved(packed(piece_rows(cells, high, (0, SHIFT)), 12), c_ref, c2_ref)
    d_ref[...] = packed(piece_rows(cells, low, (0, SHIFT)), 9)


def join_kernel(a_ref, d_ref, c_ref, c2_ref, b_ref, b2_ref, out_ref):
    a = a_ref[...].astype(F32)
    b = unpacked(whole_of(b_ref, b2_ref), 12)
    c = unpacked(whole_of(c_ref, c2_ref), 12)
    d = unpacked(d_ref, 9)
    for i in range(WIN):
        if i < SHIFT:
            left, right, k = d, b, i
        else:
            left, right, k = c, a, i - SHIFT
        rows = [left[SHIFT * k : SHIFT * k + SHIFT], right[KEEP * k : KEEP * k + KEEP]]
        out_ref[i] = jnp.concatenate(rows, axis=0).astype(BF)


def selector():
    token = lax.broadcasted_iota(jnp.int32, (1, LANES), 1)
    column = (token * 1338) >> 16
    cell = token - 49 * column
    slot = 64 * column + cell + 4 * (cell >= 28).astype(jnp.int32) + 4 * (cell >= 40).astype(jnp.int32)
    slot = jnp.where(token < TOKENS, slot, -1)
    place = lax.broadcasted_iota(jnp.int32, (WIN * SLOTS, LANES), 0)
    return (place == slot).astype(F32).astype(BF)


def by_slots(values):
    cells = [values[d] for d in range(WIN)]
    low, high = range(KEEP), range(KEEP, WIN)
    return jnp.concatenate(
        [
            piece_rows(cells, low, (0, KEEP)),
            piece_rows(cells, high, (0, KEEP)),
            piece_rows(cells, low, (KEEP, WIN)),
            piece_rows(cells, high, (KEEP, WIN)),
        ],
        axis=0,
    )


def turned(values):
    return values.astype(F32).T.astype(BF)


def ready_kernel(
    region_ref, labels_ref, g1_ref, g2_ref, qkv_ref, proj_ref, up_ref, downt_ref, head_ref,
    ids_ref, sel_ref, gain1_ref, gain2_ref, qkvt_ref, projt_ref, upt_ref, down_ref, headt_ref, heads_ref,
):
    sel = selector()
    sel_ref[...] = sel
    rows = []
    for ref in (region_ref, labels_ref):
        flat = by_slots(ref[...].astype(F32)).T
        for w in range(WINDOWS):
            rows.append(jnp.concatenate([flat[WIN * w + c : WIN * w + c + 1] for c in range(WIN)], axis=1))
    ids = nn(jnp.concatenate(rows, axis=0).astype(BF), sel)
    token = lax.broadcasted_iota(jnp.int32, ids.shape, 1)
    row = lax.broadcasted_iota(jnp.int32, ids.shape, 0)
    ids_ref[...] = jnp.where(token < TOKENS, ids, jnp.where(row < WINDOWS, 4.0, -1.0))
    for ref, out in ((g1_ref, gain1_ref), (g2_ref, gain2_ref)):
        out[...] = jnp.broadcast_to(ref[...], (128, C)).T
    qkvt_ref[...] = turned(qkv_ref[...])
    projt_ref[...] = turned(proj_ref[...])
    upt_ref[...] = turned(up_ref[...])
    down_ref[...] = turned(downt_ref[...])
    head = jnp.concatenate([head_ref[...].astype(F32), jnp.zeros((2, C), F32)], axis=0)
    headt_ref[...] = head.astype(BF)
    heads_ref[...] = head.T.astype(BF)


def norm(values, gain):
    center = values - jnp.mean(values, axis=0, keepdims=True)
    inverse = lax.rsqrt(jnp.mean(center * center, axis=0, keepdims=True) + 1e-5)
    unit = center * inverse
    return unit, inverse, (unit * gain).astype(BF)


def norm_back(cotangent, unit, inverse, gain):
    scaled = cotangent * gain
    middle = jnp.mean(scaled, axis=0, keepdims=True)
    along = jnp.mean(scaled * unit, axis=0, keepdims=True)
    return inverse * (scaled - middle - unit * along)


def paired(rows, first, second):
    blank = jnp.zeros((HEAD, LANES), BF)
    left = jnp.concatenate([rows[:HEAD], blank, first], axis=0)
    right = jnp.concatenate([blank, rows[HEAD:], second], axis=0)
    return jnp.concatenate([left, right], axis=1)


def blockdiag(rows):
    blank = jnp.zeros((HEAD, LANES), BF)
    first = jnp.concatenate([rows[:HEAD], blank], axis=1)
    second = jnp.concatenate([blank, rows[HEAD:]], axis=1)
    return jnp.concatenate([first, second], axis=0)


def by_columns(rows, weights):
    rows = rows[:, :ROWS]
    left = nn(rows[:HEAD], weights[:, :256])
    middle = nn(rows, weights[:, 256:512])
    right = nn(rows[HEAD:], weights[:, 512:])
    first = jnp.concatenate([left, middle[:HEAD, :128]], axis=1)
    second = jnp.concatenate([middle[HEAD:, 128:], right], axis=1)
    return jnp.concatenate([first, second], axis=0)


def across(ref):
    columns = []
    for w in range(WINDOWS):
        columns.append(jnp.concatenate([ref[PAIRS * w + p] for p in range(PAIRS)], axis=0))
    return jnp.concatenate(columns, axis=1)


def each_pair(values):
    for w in range(WINDOWS):
        for p in range(PAIRS):
            yield PAIRS * w + p, values[32 * p : 32 * p + 32, LANES * w : LANES * w + LANES]


def in_turn(start, finish, buffers):
    first, second = buffers
    last = WINDOWS * PAIRS - 2

    def two(i, carry):
        start(2 * i + 1, *second)
        finish(2 * i, *first)
        start(2 * i + 2, *first)
        finish(2 * i + 1, *second)
        return carry

    start(0, *first)
    lax.fori_loop(0, last // 2, two, 0, unroll=5)
    start(last + 1, *second)
    finish(last, *first)
    finish(last + 1, *second)


def main_kernel(
    scale,
    a_ref, d_ref, c_ref, c2_ref, b_ref, b2_ref, ids_ref, sel_ref, gain1_ref, gain2_ref,
    qkv_ref, qkvt_ref, proj_ref, projt_ref, up_ref, upt_ref, down_ref, downt_ref, head_ref, headt_ref,
    oa_ref, od_ref, oc_ref, oc2_ref, ob_ref, ob2_ref,
    x_ref, unit1_ref, inverse1_ref, q_ref, k_ref, v_ref, keyst_ref, valuest_ref, side_ref, e_ref, s0_ref, s1_ref, top0_ref, top1_ref,
    attended_ref, inverse_ref, d_hidden_ref, d_mixed_ref, extra_ref, dq_ref, dk_ref, dv_ref, slope_ref,
):
    sel = sel_ref[...]
    pieces = [a_ref[...].astype(F32), unpacked(whole_of(b_ref, b2_ref), 12), unpacked(whole_of(c_ref, c2_ref), 12), unpacked(d_ref, 9)]
    rows = jnp.concatenate(pieces, axis=0)
    tall = rows.T
    wides = []
    for w in range(WINDOWS):
        cols = [(WIN * w + SHIFT + c) % NX for c in range(WIN)]
        wides.append(jnp.concatenate([tall[C * c : C * c + C] for c in cols], axis=1).astype(BF))
    stacked = nn(jnp.concatenate(wides, axis=0), sel)
    x = jnp.concatenate([stacked[C * w : C * w + C] for w in range(WINDOWS)], axis=1)
    x_ref[...] = x
    dk_ref[...] = jnp.zeros(dk_ref.shape, BF)
    dv_ref[...] = jnp.zeros(dv_ref.shape, BF)

    gain1 = jnp.concatenate([gain1_ref[...]] * (3 * WINDOWS), axis=1)
    gain2 = jnp.concatenate([gain2_ref[...]] * (3 * WINDOWS), axis=1)
    unit1, inverse1, normed1 = norm(x, gain1)
    unit1_ref[...] = unit1
    inverse1_ref[0:1, :] = inverse1
    index = lax.broadcasted_iota(jnp.int32, (16, LANES), 0)
    ones = jnp.where(index < 2, 1.0, 0.0).astype(BF)
    key_sides = []
    for w in range(WINDOWS):
        same = index.astype(F32) == ids_ref[w : w + 1, :]
        key_sides.append(same.astype(F32).astype(BF))
        side_ref[w] = jnp.where(same | (index > 4), 0.0, FAR).astype(BF)
    for t, part in each_pair((nn(qkvt_ref[:C, :], normed1) * (0.25 * LOG2E)).astype(BF)):
        q_ref[t] = part
    for t, part in each_pair(nn(qkvt_ref[C : 2 * C, :], normed1).astype(BF)):
        k_ref[t] = part
        keyst_ref[t] = turned(jnp.concatenate([part, key_sides[t // PAIRS]], axis=0))[:ROWS]
    for t, part in each_pair(nn(qkvt_ref[2 * C :, :], normed1).astype(BF)):
        v_ref[t] = part
        valuest_ref[t] = turned(jnp.concatenate([part, ones], axis=0))[:ROWS]

    def score(t, out_ref, top_ref):
        side = side_ref[lax.div(t, PAIRS)]
        scores = nn(keyst_ref[t], paired(q_ref[t], side, side))
        out_ref[...] = scores
        top_ref[0:1, :] = jnp.max(scores, axis=0, keepdims=True)

    def mix(t, in_ref, top_ref):
        powers = jnp.exp2(in_ref[...] - top_ref[0:1, :])
        raised = powers.astype(BF)
        e_ref[t] = raised
        inverse_sum = 1.0 / jnp.sum(powers, axis=0, keepdims=True)
        sums = []
        for h in range(2):
            part = inverse_sum[:, LANES * h : LANES * h + LANES]
            inverse_ref[t, h : h + 1, :] = part
            sums.append(jnp.broadcast_to(part, (HEAD, LANES)))
        attended_ref[t] = (by_columns(v_ref[t], raised) * jnp.concatenate(sums, axis=0)).astype(BF)

    buffers = ((s0_ref, top0_ref), (s1_ref, top1_ref))
    in_turn(score, mix, buffers)

    attended = across(attended_ref)
    hidden = x_ref[...] + nn(projt_ref[...], attended)
    unit2, inverse2, normed2 = norm(hidden, gain2)
    output = hidden
    for j in range(3):
        part = slice(128 * j, 128 * j + 128)
        raised = nn(upt_ref[part, :], normed2)
        inner = raised * (0.5**0.5)
        below = 0.5 + 0.5 * lax.erf(inner)
        bell = jnp.exp2(inner * inner * -LOG2E)
        slope_ref[part, :] = below + (raised * 0.3989422804014327) * bell
        output = output + nn(downt_ref[:, part], (raised * below).astype(BF))
    logits = nn(headt_ref[...], output.astype(BF))
    labels = jnp.concatenate([ids_ref[WINDOWS + w : WINDOWS + w + 1, :] for w in range(WINDOWS)], axis=1)
    kind = lax.broadcasted_iota(jnp.int32, (16, WINDOWS * LANES), 0)
    logits = jnp.where(kind < CLASSES, logits, -1e30)
    powers = jnp.exp(logits - jnp.max(logits, axis=0, keepdims=True))
    soft = powers / jnp.sum(powers, axis=0, keepdims=True)
    at_label = (kind.astype(F32) == labels).astype(F32)
    d_logits = jnp.where(labels >= 0.0, (soft - at_label) * scale, 0.0)
    d_output = nn(head_ref[...], d_logits.astype(BF)).astype(BF)
    d_normed2 = jnp.zeros((C, WINDOWS * LANES), F32)
    for j in range(3):
        part = slice(128 * j, 128 * j + 128)
        d_expanded = nn(down_ref[part, :], d_output)
        d_raised = (d_expanded * slope_ref[part, :]).astype(BF)
        d_normed2 = d_normed2 + nn(up_ref[:, part], d_raised)
    d_hidden = d_output.astype(F32) + norm_back(d_normed2, unit2, inverse2, gain2)
    d_hidden_ref[...] = d_hidden
    d_attended = nn(proj_ref[...], d_hidden.astype(BF))
    for h in range(HEADS):
        own = slice(HEAD * h, HEAD * h + HEAD)
        sums = jnp.concatenate(
            [inverse_ref[PAIRS * w + h // 2, h % 2 : h % 2 + 1, :] for w in range(WINDOWS)], axis=1
        )
        d_mixed = (d_attended[own] * sums).astype(BF)
        along = -jnp.sum(d_mixed.astype(F32) * attended[own].astype(F32), axis=0, keepdims=True)
        coarse = along.astype(BF).astype(F32)
        rest = along - coarse
        place = slice(HEAD * (h % 2), HEAD * (h % 2) + HEAD)
        for w in range(WINDOWS):
            lanes = slice(LANES * w, LANES * w + LANES)
            d_mixed_ref[PAIRS * w + h // 2, place, :] = d_mixed[:, lanes]
            extra = jnp.where(index == 0, coarse[:, lanes], jnp.where(index == 1, rest[:, lanes], 0.0))
            extra_ref[PAIRS * w + h // 2, place, :] = extra.astype(BF)

    def weigh(t, out_ref, unused):
        extra = extra_ref[t]
        out_ref[...] = nn(valuest_ref[t], paired(d_mixed_ref[t], extra[:HEAD], extra[HEAD:]))

    def unmix(t, in_ref, unused):
        raised = e_ref[t]
        d_scores = (raised.astype(F32) * in_ref[...]).astype(BF)
        dv_ref[t, :, :ROWS] = nt(blockdiag(d_mixed_ref[t]), raised).astype(BF)
        dq_ref[t] = (by_columns(k_ref[t], d_scores) * 0.25).astype(BF)
        dk_ref[t, :, :ROWS] = (nt(d_scores, blockdiag(q_ref[t])).T * LN2).astype(BF)

    in_turn(weigh, unmix, buffers)

    d_normed1 = nn(qkv_ref[...], jnp.concatenate([across(r) for r in (dq_ref, dk_ref, dv_ref)], axis=0))
    unit1, inverse1 = unit1_ref[...], inverse1_ref[0:1, :]
    grad = (d_hidden_ref[...] + norm_back(d_normed1, unit1, inverse1, gain1)).astype(BF)
    blocks = [None] * NX
    stacked = nt(jnp.concatenate([grad[:, LANES * w : LANES * w + LANES] for w in range(WINDOWS)], axis=0), sel)
    for w in range(WINDOWS):
        wide = stacked[C * w : C * w + C]
        for c in range(WIN):
            blocks[(WIN * w + SHIFT + c) % NX] = wide[:, SLOTS * c : SLOTS * c + SLOTS]
    rows = jnp.concatenate(blocks, axis=0).T
    oa_ref[...] = rows[:16].astype(BF)
    halved(packed(rows[16:32], 12), ob_ref, ob2_ref)
    halved(packed(rows[32:48], 12), oc_ref, oc2_ref)
    od_ref[...] = packed(rows[48:], 9)


VMEM = pl.BlockSpec(memory_space=pltpu.VMEM)
SMALL = pltpu.CompilerParams(vmem_limit_bytes=8 * 2**20)
PIECES = [jax.ShapeDtypeStruct(s, BF) for s in ((16, WIDE), (8, 3072), (8, 2048), (8, 2048), (8, 2048), (8, 2048))]


def cut(features):
    return pl.pallas_call(cut_kernel, out_shape=PIECES, in_specs=[VMEM], out_specs=[VMEM] * 6, compiler_params=SMALL)(features)


def join(*pieces):
    out = jax.ShapeDtypeStruct((WIN, WIN, WIDE), BF)
    return pl.pallas_call(join_kernel, out_shape=out, in_specs=[VMEM] * 6, out_specs=VMEM, compiler_params=SMALL)(*pieces)


def ready(region, labels, attn_gain, mlp_gain, qkv_weight, proj_weight, up_weight, down_weight, head_weight):
    S = jax.ShapeDtypeStruct
    out = [
        S((8, LANES), F32), S((WIN * SLOTS, LANES), BF), S((C, 128), F32), S((C, 128), F32),
        S((3 * C, C), BF), S((C, C), BF), S((HID, C), BF), S((HID, C), BF), S((16, C), BF), S((C, 16), BF),
    ]
    return pl.pallas_call(ready_kernel, out_shape=out, in_specs=[VMEM] * 9, out_specs=[VMEM] * 10, compiler_params=SMALL)(
        region, labels, attn_gain.reshape(1, C), mlp_gain.reshape(1, C),
        qkv_weight, proj_weight, up_weight, down_weight, head_weight,
    )


def gradient(pieces, prepared, weights, scale):
    ids, sel, gain1, gain2, qkv_t, proj_t, up_t, down, head_t, head = prepared
    qkv_weight, proj_weight, up_weight, down_t = weights
    return pl.pallas_call(
        functools.partial(main_kernel, scale),
        out_shape=PIECES,
        in_specs=[VMEM] * 20,
        out_specs=[VMEM] * 6,
        scratch_shapes=[
            pltpu.VMEM((C, WINDOWS * LANES), F32),
            pltpu.VMEM((C, WINDOWS * LANES), F32),
            pltpu.VMEM((8, WINDOWS * LANES), F32),
            pltpu.VMEM((12, 32, LANES), BF),
            pltpu.VMEM((12, 32, LANES), BF),
            pltpu.VMEM((12, 32, LANES), BF),
            pltpu.VMEM((12, ROWS, 48), BF),
            pltpu.VMEM((12, ROWS, 48), BF),
            pltpu.VMEM((WINDOWS, 16, LANES), BF),
            pltpu.VMEM((12, ROWS, 2 * LANES), BF),
            pltpu.VMEM((ROWS, 2 * LANES), F32),
            pltpu.VMEM((ROWS, 2 * LANES), F32),
            pltpu.VMEM((8, 2 * LANES), F32),
            pltpu.VMEM((8, 2 * LANES), F32),
            pltpu.VMEM((12, 32, LANES), BF),
            pltpu.VMEM((12, 8, LANES), F32),
            pltpu.VMEM((C, WINDOWS * LANES), F32),
            pltpu.VMEM((12, 32, LANES), BF),
            pltpu.VMEM((12, 32, LANES), BF),
            pltpu.VMEM((12, 32, LANES), BF),
            pltpu.VMEM((12, 32, LANES), BF),
            pltpu.VMEM((12, 32, LANES), BF),
            pltpu.VMEM((HID, WINDOWS * LANES), F32),
        ],
        compiler_params=pltpu.CompilerParams(vmem_limit_bytes=32 * 2**20),
    )(
        *pieces, ids, sel, gain1, gain2, qkv_weight, qkv_t, proj_weight, proj_t,
        up_weight, up_t, down, down_t, head, head_t,
    )


def moved(piece, axes, steps):
    sizes = [lax.axis_size(a) for a in axes]
    route = []
    if len(axes) == 1:
        (n,) = sizes
        route = [((i - steps) % n, i) for i in range(n)]
    else:
        n, m = sizes
        for i in range(n):
            for j in range(m):
                route.append((((i - steps) % n) * m + (j - steps) % m, i * m + j))
    return lax.ppermute(piece, axes if len(axes) > 1 else axes[0], route)


ROADS = (("gz", "gy"), ("gy",), ("gy",), ("gz",), ("gz",))


def body(
    features, region, labels, attn_gain, qkv_weight, proj_weight, mlp_gain, up_weight, down_weight, head_weight,
):
    own, *away = cut(features)
    down_t = down_weight.T
    arrived = [moved(piece, road, -1) for piece, road in zip(away, ROADS)]
    prepared = ready(
        region, labels, attn_gain, mlp_gain, qkv_weight, proj_weight, up_weight, down_t, head_weight.T
    )
    scale = 1.0 / (WIN * WIN * NX * lax.axis_size("gz") * lax.axis_size("gy"))
    own, *away = gradient((own, *arrived), prepared, (qkv_weight, proj_weight, up_weight, down_t), scale)
    arrived = [moved(piece, road, 1) for piece, road in zip(away, ROADS)]
    return join(own, *arrived)


def solution(mesh):
    cells = P("gz", "gy", None)
    in_specs = (cells, cells, cells) + (P(),) * 7
    return jax.shard_map(body, mesh=mesh, in_specs=in_specs, out_specs=cells, check_vma=False)
```
